32 devices in a mesh: tier: 2 (over x), row: 16 (over z, y, core).
Axes of the slice: x: 2, y: 2, z: 4, core: 2. Of those that a mesh axis runs over, the one named last changes fastest.
Arguments:
- current_modes: float32 [8192, 128], P(('tier', 'row')), may hold values from -6 to 6
- previous: float32 [8192, 128], P(('tier', 'row')), may hold values from -4 to 4
- diag_tiles: bfloat16 [2, 16, 2, 128, 128], P('tier', 'row'), may hold values from -2 to 8, as said below
- lateral_tiles: bfloat16 [2, 16, 2, 2, 128, 128], P('tier', 'row'), may hold values from -0.25 to 0.25
- lateral_index: int32 [2, 16, 2, 2], P('tier', 'row'), may hold values from 0 to 3, as said below
- vertical_tiles: bfloat16 [2, 16, 2, 128, 128], P('tier', 'row'), may hold values from -0.5 to 0.5
- vertical_index: int32 [2, 16, 2], P('tier', 'row'), may hold values from 0 to 1, each once within a row
- smoother: float32 [2, 16, 2, 128, 128], P('tier', 'row'), may hold values from -1 to 2
Outputs:
- ortho_basis: float32 [8192, 384], P(('tier', 'row'))
- projected: float32 [384, 384], replicated
The draws below stay inside these ranges and needn't reach their ends.
Inputs may be any that keep to these rules, and one draw needn't show every extreme that they name: lateral_index[t,r,g,0] lies in 0 to g and lateral_index[t,r,g,1] in g+2 to 3; slot 0 is the last tile of the previous row block, slots 1 to 2 this block's tiles, slot 3 the first tile of the next row block. `vertical_index`: the entries of one row block form a permutation of its tiles. `diag_tiles`: each tile is symmetric.
All inputs are finite; a program needn't handle non-finite values.
Results may differ from the reference program's by a relative error of at most 0.0015.
The reference program's roundings to bfloat16 on the way count: a program that leaves them out, or rounds other values in their place, can miss the bound.
Values may be sent and summed in bfloat16 or wider, within the bound.
A program may use at most 64 MiB of HBM per device.

```python
import jax
import jax.numpy as jnp
from jax import lax

K = 128
BT = 128
RT = 2
NTIER = 2
NROW = 16
ROWS = 8192


def draw_diag_tiles(key, part):
    key = jax.random.fold_in(key, 11)
    first_key, second_key = jax.random.split(key)
    full_shape = (NTIER, NROW, RT, BT, BT)
    levels = jax.random.uniform(first_key, full_shape[:-1], jnp.float32, 2.0, 5.0)
    jitter = jnp.clip(jax.random.normal(second_key, full_shape, jnp.float32), -4.0, 4.0) * (0.35 / BT) ** 0.5
    mirrored = jitter + jnp.swapaxes(jitter, -1, -2)
    identity = jnp.eye(BT, dtype=jnp.float32)
    return (mirrored + identity * levels[..., None, :]).astype(jnp.bfloat16)


def draw_smoother(key, part):
    key = jax.random.fold_in(key, 23)
    first_key, second_key = jax.random.split(key)
    full_shape = (NTIER, NROW, RT, BT, BT)
    levels = jax.random.uniform(first_key, full_shape[:-1], jnp.float32, 0.5, 1.0)
    jitter = jnp.clip(jax.random.normal(second_key, full_shape, jnp.float32), -4.0, 4.0) * (0.03 / BT) ** 0.5
    mirrored = jitter + jnp.swapaxes(jitter, -1, -2)
    identity = jnp.eye(BT, dtype=jnp.float32)
    return mirrored + identity * levels[..., None, :]


def draw_lateral_index(key, part):
    key = jax.random.fold_in(key, 37)
    first_key, second_key = jax.random.split(key)
    full_shape = (NTIER, NROW, RT)
    column = jnp.arange(RT, dtype=jnp.int32)
    lower_pick = jax.random.randint(first_key, full_shape, 0, 1 << 20, dtype=jnp.int32) % (column + 1)
    upper_pick = column + 2 + jax.random.randint(second_key, full_shape, 0, 1 << 20, dtype=jnp.int32) % (RT - column)
    return jnp.stack([lower_pick, upper_pick], -1)


def level_of(rng, shape, cuts, smallest, high):
    factor_of, own = 1.0, jax.random.fold_in(rng, 6)
    for axis_at, parts in cuts:
        steps = jnp.exp(jax.random.uniform(jax.random.fold_in(own, axis_at), (parts,), jnp.float32, smallest / len(cuts), high / len(cuts)))
        factor_of = factor_of * jnp.repeat(steps, shape[axis_at] // parts).reshape([-1 if axis == axis_at else 1 for axis in range(len(shape))])
    return factor_of


def bell_draw(key, extent, width, reach, cuts=(), kind=jnp.bfloat16):
    loudness = level_of(key, extent, cuts, -0.22, 0.18) if cuts else 1.0
    entries = jax.random.normal(key, extent, jnp.float32) * width * loudness
    return jnp.minimum(jnp.maximum(entries, -reach), reach).astype(kind)


def setup_inputs(seed: int = 0) -> dict:
    key_of = jax.random.split(jax.random.key(seed), 9)
    return {
        "current_modes": bell_draw(key_of[0], (ROWS, K), 1.0, 6.0, ((0, 32),), jnp.float32),
        "previous": bell_draw(key_of[1], (ROWS, K), 0.5, 4.0, ((0, 32),), jnp.float32),
        "diag_tiles": draw_diag_tiles(jax.random.fold_in(key_of[8], 71), 0),
        "lateral_tiles": bell_draw(key_of[3], (NTIER, NROW, RT, 2, BT, BT), (4 * BT) ** -0.5, 0.25, ((0, 2), (1, 16))),
        "lateral_index": draw_lateral_index(jax.random.fold_in(key_of[8], 71), 0),
        "vertical_tiles": bell_draw(key_of[5], (NTIER, NROW, RT, BT, BT), BT ** -0.5, 0.5, ((0, 2), (1, 16))),
        "vertical_index": jax.vmap(lambda own: jax.random.permutation(own, RT))(jax.random.split(key_of[6], NTIER * NROW)).reshape((NTIER, NROW, RT)).astype(jnp.int32),
        "smoother": draw_smoother(jax.random.fold_in(key_of[8], 71), 0),
    }


def as_float(array):
    return array.astype(jnp.float32)

def tier_image(inputs):
    values, lower_values, upper_values, diag_part, side_part, side_slots, down_part, down_slots, up_part, up_slots = inputs
    own_tiles = as_float(values)
    column_count = own_tiles.shape[-1]
    result = jnp.einsum('rjik,rjkc->rjic', as_float(diag_part), own_tiles)
    flat_tiles = own_tiles.reshape(NROW * RT, BT, column_count)
    border = jnp.zeros((1, BT, column_count), jnp.float32)
    padded = jnp.concatenate([border, flat_tiles, border], 0)
    global_slot = (jnp.arange(NROW, dtype=jnp.int32) * RT)[:, None, None] + side_slots
    result = result + jnp.einsum('rjbik,rjbkc->rjic', as_float(side_part), padded[global_slot])
    mirror = jnp.einsum('rjbki,rjkc->rjbic', as_float(side_part), own_tiles)
    spread = jnp.zeros_like(padded).at[global_slot.reshape(-1)].add(mirror.reshape(-1, BT, column_count))
    result = result + spread[1:-1].reshape(NROW, RT, BT, column_count)
    pulled = jnp.take_along_axis(as_float(lower_values), down_slots[:, :, None, None], axis=1)
    result = result + jnp.einsum('rjik,rjkc->rjic', as_float(down_part), pulled)
    lifted = jnp.einsum('rkij,rkic->rkjc', as_float(up_part), as_float(upper_values))
    block_index = jnp.broadcast_to(jnp.arange(NROW, dtype=jnp.int32)[:, None], up_slots.shape)
    result = result + jnp.zeros_like(result).at[block_index, up_slots].add(lifted)
    return result

def apply_operator(values, diag_tiles, lateral_tiles, lateral_index, vertical_tiles, vertical_index):
    column_count = values.shape[-1]
    layered = values.reshape(NTIER, NROW, RT, BT, column_count)
    empty_layer = jnp.zeros_like(layered[:1])
    lower_values = jnp.concatenate([empty_layer, layered[:-1]], 0)
    upper_values = jnp.concatenate([layered[1:], empty_layer], 0)
    upper_tiles = jnp.concatenate([vertical_tiles[1:], jnp.zeros_like(vertical_tiles[:1])], 0)
    upper_slots = jnp.concatenate([vertical_index[1:], jnp.zeros_like(vertical_index[:1])], 0)
    images = lax.map(tier_image, (layered, lower_values, upper_values, diag_tiles, lateral_tiles, lateral_index, vertical_tiles, vertical_index, upper_tiles, upper_slots))
    return images.reshape(NTIER * NROW * RT * BT, column_count)

def right_solve(factor, matrix):
    return jax.scipy.linalg.solve_triangular(factor, matrix.T, lower=True).T

def reference(current_modes, previous, diag_tiles, lateral_tiles, lateral_index, vertical_tiles, vertical_index, smoother):
    highest = lax.Precision.HIGHEST
    paired = apply_operator(jnp.concatenate([current_modes, previous], 1).astype(jnp.bfloat16), diag_tiles, lateral_tiles, lateral_index, vertical_tiles, vertical_index)
    mode_image = paired[:, :K]
    prev_image = paired[:, K:]
    quotient = jnp.sum(current_modes * mode_image, 0) / jnp.sum(current_modes * current_modes, 0)
    residue = (mode_image - current_modes * quotient).reshape(NTIER, NROW, RT, BT, K)
    lower_field = jnp.zeros_like(residue[0])
    layers = []
    for tier_number in range(NTIER):
        pulled = jnp.take_along_axis(lower_field, vertical_index[tier_number][:, :, None, None], axis=1)
        coupled = jnp.einsum('rjik,rjkc->rjic', as_float(vertical_tiles[tier_number]), pulled, precision=highest)
        lower_field = jnp.einsum('rjik,rjkc->rjic', smoother[tier_number], residue[tier_number] - coupled, precision=highest)
        layers.append(lower_field)
    precond = jnp.stack(layers).reshape(ROWS, K)
    work_image = apply_operator(precond.astype(jnp.bfloat16), diag_tiles, lateral_tiles, lateral_index, vertical_tiles, vertical_index)
    stacked = jnp.concatenate([current_modes, precond, previous], 1)
    images = jnp.concatenate([mode_image, work_image, prev_image], 1)
    factor = jnp.linalg.cholesky(jnp.dot(stacked.T, stacked, precision=highest) / ROWS)
    ortho_basis = right_solve(factor, stacked)
    mapped = right_solve(factor, images)
    projected = jnp.dot(ortho_basis.T, mapped, precision=highest) / ROWS
    return (ortho_basis, projected)
```

```python
import functools

import jax
import jax.numpy as jnp
from jax import lax
from jax.experimental import pallas as pl
from jax.experimental.pallas import tpu as pltpu
from jax.sharding import PartitionSpec as P

F32 = jnp.float32
BF16 = jnp.bfloat16
MESH = pl.DeviceIdType.MESH


def dot(a, b):
    return jnp.dot(a, b, preferred_element_type=F32)


def dot_t(a, b):
    return lax.dot_general(a, b, (((0,), (0,)), ((), ())), preferred_element_type=F32)


def halves(x):
    high = x.astype(BF16)
    return high, (x - high.astype(F32)).astype(BF16)


def dot3(a, b, product=dot):
    (a_high, a_low), (b_high, b_low) = halves(a), halves(b)
    return product(a_high, b_high) + (product(a_high, b_low) + product(a_low, b_high))


def flag(condition):
    return jnp.where(condition, 1.0, 0.0).astype(F32)


def scaled(tile, factor):
    return (tile.astype(F32) * factor).astype(BF16)


F_PREV, F_NEXT, F_LOW, F_UP, T_PREV, T_NEXT, T_LOW, P_UP, W_PREV, W_NEXT, W_LOW, W_UP, QUOT = range(13)
SUM_AT, SHARE_AT = 13, 16
SEMS = 19


def step_kernel(
    tiers, rows, cuts,
    cm, pv, diag, lat, lat_at, vert, vert_at, smo,
    w_out, early, mid, late,
    f_own, f_prev, f_next, f_low, f_up,
    t_prev, t_next, t_low, got_prev, got_next, got_up,
    p_own, p_low, wb, wb_prev, wb_next, wb_low, wb_up,
    q_buf, src0, src1, src2, box0, box1, box2,
    send_sem, recv_sem,
):
    tier, row = lax.axis_index("tier"), lax.axis_index("row")
    count = tiers * rows
    me = tier * rows + row
    bt = diag.shape[-1]
    k = cm.shape[1]

    def place(d):
        return (lax.div(d, rows), lax.rem(d, rows))

    def others(body):
        def step(i, carry):
            body(lax.rem(me + i, count))
            return carry
        lax.fori_loop(1, count, step, 0)

    barrier = pltpu.get_barrier_semaphore()
    others(lambda d: pl.semaphore_signal(barrier, inc=1, device_id=place(d), device_id_type=MESH))

    def remote(src, dst, slot, device):
        return pltpu.make_async_remote_copy(
            src_ref=src, dst_ref=dst, send_sem=send_sem.at[slot], recv_sem=recv_sem.at[slot],
            device_id=device, device_id_type=MESH)

    has_prev, has_next = row > 0, row < rows - 1
    has_low, has_up = tier > 0, tier < tiers - 1
    PREV, NEXT = (has_prev, has_next, (tier, row - 1)), (has_next, has_prev, (tier, row + 1))
    LOW, UP = (has_low, has_up, (tier - 1, row)), (has_up, has_low, (tier + 1, row))

    def send(src, dst, slot, way):
        @pl.when(way[0])
        def _():
            remote(src, dst, slot, way[2]).start()

    def receive(src, dst, slot, way):
        @pl.when(way[1])
        def _():
            remote(src, dst, slot, (tier, row)).wait_recv()

    def sent(src, dst, slot, way):
        @pl.when(way[0])
        def _():
            remote(src, dst, slot, (tier, row)).wait_send()

    f_own[:, :k] = cm[...].astype(BF16)
    f_own[:, k:] = pv[...].astype(BF16)
    below = flag(lat_at[1, 0] == 0)
    inner_low = 1.0 - below
    above = flag(lat_at[0, 1] == 3)
    inner_up = 1.0 - above
    t_prev[:bt] = lat[0, 0]
    t_prev[bt:] = scaled(lat[1, 0], below)
    t_next[:bt] = scaled(lat[0, 1], above)
    t_next[bt:] = lat[1, 1]
    for g in range(2):
        swap = flag(vert_at[g] == 1)
        t_low[g * bt:(g + 1) * bt, :bt] = scaled(vert[g], 1.0 - swap)
        t_low[g * bt:(g + 1) * bt, bt:] = scaled(vert[g], swap)

    @pl.when(jnp.logical_not(has_prev))
    def _():
        f_prev[...] = jnp.zeros_like(f_prev)
        wb_prev[...] = jnp.zeros_like(wb_prev)
        got_prev[...] = jnp.zeros_like(got_prev)

    @pl.when(jnp.logical_not(has_next))
    def _():
        f_next[...] = jnp.zeros_like(f_next)
        wb_next[...] = jnp.zeros_like(wb_next)
        got_next[...] = jnp.zeros_like(got_next)

    @pl.when(jnp.logical_not(has_low))
    def _():
        f_low[...] = jnp.zeros_like(f_low)
        wb_low[...] = jnp.zeros_like(wb_low)
        p_low[...] = jnp.zeros_like(p_low)

    @pl.when(jnp.logical_not(has_up))
    def _():
        f_up[...] = jnp.zeros_like(f_up)
        wb_up[...] = jnp.zeros_like(wb_up)
        got_up[...] = jnp.zeros_like(got_up)

    first = [
        (f_own, f_up, F_LOW, LOW), (f_own, f_low, F_UP, UP),
        (f_own, f_next, F_PREV, PREV), (f_own, f_prev, F_NEXT, NEXT),
        (t_low, got_up, T_LOW, LOW), (t_prev, got_next, T_PREV, PREV), (t_next, got_prev, T_NEXT, NEXT),
    ]
    second = [
        (wb, wb_up, W_LOW, LOW), (wb, wb_low, W_UP, UP),
        (wb, wb_next, W_PREV, PREV), (wb, wb_prev, W_NEXT, NEXT),
    ]
    pl.semaphore_wait(barrier, count - 1)
    for item in first:
        send(*item)

    zero = jnp.zeros((bt, bt), BF16)
    cross_up, cross_low = scaled(lat[0, 1], inner_up), scaled(lat[1, 0], inner_low)
    inner = jnp.concatenate([
        jnp.concatenate([diag[0], cross_up], 1), jnp.concatenate([cross_low, diag[1]], 1)], 0)
    crossed = jnp.concatenate([
        jnp.concatenate([zero, cross_up], 1), jnp.concatenate([cross_low, zero], 1)], 0)

    def local(own):
        return dot(inner, own) + dot_t(crossed, own)

    def coupled(total, prev, after, low, up):
        total = total + dot(t_prev[...], prev[bt:]) + dot(t_next[...], after[:bt])
        total = total + dot(t_low[...], low[...]) + dot_t(got_up[...], up[...])
        edge = jnp.concatenate([dot_t(got_prev[...], prev[...]), dot_t(got_next[...], after[...])], 0)
        return total + edge

    def spread(src, box, which):
        chunk, owners = cuts[which]
        def body(d):
            @pl.when(d < owners)
            def _():
                remote(src.at[pl.ds(pl.multiple_of(d * chunk, 8), chunk)], box.at[me], SUM_AT + which, place(d)).start()
        others(body)
        @pl.when(me < owners)
        def _():
            box[pl.ds(me, 1)] = src[pl.ds(pl.multiple_of(me * chunk, 8), chunk)][None]

    def share(src, box, out, which):
        chunk, owners = cuts[which]
        @pl.when(me < owners)
        def _():
            everything = box.at[pl.ds(0, count - 1)]
            remote(everything, everything, SUM_AT + which, (tier, row)).wait_recv()
            mine = pl.ds(pl.multiple_of(me * chunk, 8), chunk)
            out[mine] = jnp.sum(box[...], axis=0)
            others(lambda d: remote(out.at[mine], out.at[mine], SHARE_AT + which, place(d)).start())

    def gathered(src, box, out, which):
        chunk, owners = cuts[which]
        def arrive(number):
            part = out.at[pl.ds(0, number * chunk)]
            remote(part, part, SHARE_AT + which, (tier, row)).wait_recv()
            part = src.at[pl.ds(0, number * chunk)]
            remote(part, part, SUM_AT + which, (tier, row)).wait_send()
        @pl.when(me < owners)
        def _():
            arrive(owners - 1)
            everything = box.at[pl.ds(0, count - 1)]
            remote(everything, everything, SHARE_AT + which, (tier, row)).wait_send()
        @pl.when(me >= owners)
        def _():
            arrive(owners)

    total = local(f_own[...])
    for item in first:
        receive(*item)
    image = coupled(total, f_prev, f_next, f_low, f_up)
    x, mode_image = cm[...], image[:, :k]
    q_buf[pl.ds(me, 1), 0:1] = jnp.sum(x * mode_image, 0, keepdims=True)[None]
    q_buf[pl.ds(me, 1), 1:2] = jnp.sum(x * x, 0, keepdims=True)[None]
    others(lambda d: remote(q_buf.at[me], q_buf.at[me], QUOT, place(d)).start())

    pair = jnp.concatenate([mode_image, x], 1)
    receive(p_own, p_low, P_UP, UP)
    low_high, low_low = halves(p_low[...])
    pair = pair - (dot(t_low[...], low_high) + dot(t_low[...], low_low))
    p_own[:bt] = dot3(smo[0], pair[:bt])
    p_own[bt:] = dot3(smo[1], pair[bt:])
    send(p_own, p_low, P_UP, UP)

    fields = jnp.concatenate([x, pv[...]], 1)
    given = jnp.concatenate([fields, image], 1)
    product = dot3(fields, given, dot_t)
    src0[0 * k:1 * k] = product[:k, :k]
    src0[1 * k:2 * k] = product[:k, k:2 * k]
    src0[2 * k:3 * k] = product[k:, k:2 * k]
    src0[3 * k:4 * k] = product[:k, 2 * k:3 * k]
    src0[4 * k:5 * k] = product[k:, 2 * k:3 * k]
    src0[5 * k:6 * k] = product[k:, 3 * k:]
    src1[0 * k:1 * k] = product[:k, 3 * k:]
    spread(src0, box0, 0)

    everyone = q_buf.at[pl.ds(0, count - 1)]
    remote(everyone, everyone, QUOT, (tier, row)).wait_recv()
    sums = jnp.sum(q_buf[...], axis=0)
    w = p_own[:, :k] - p_own[:, k:] * (sums[0:1] / sums[1:2])
    w_out[...] = w
    wb[...] = w.astype(BF16)
    for item in second:
        send(*item)

    product = dot3(w, jnp.concatenate([given, w], 1), dot_t)
    for at in range(5):
        src1[(at + 1) * k:(at + 2) * k] = product[:, at * k:(at + 1) * k]
    spread(src1, box1, 1)
    total = local(wb[...])
    for item in second:
        receive(*item)
    work_image = coupled(total, wb_prev, wb_next, wb_low, wb_up)
    product = dot3(jnp.concatenate([fields, w], 1), work_image, dot_t)
    src2[...] = product
    spread(src2, box2, 2)
    share(src0, box0, early, 0)
    share(src1, box1, mid, 1)
    share(src2, box2, late, 2)
    gathered(src0, box0, early, 0)
    gathered(src1, box1, mid, 1)
    gathered(src2, box2, late, 2)
    remote(everyone, everyone, QUOT, (tier, row)).wait_send()
    for item in first + second:
        sent(*item)
    sent(p_own, p_low, P_UP, UP)


def basis_kernel(
    inverse_rows, early, mid, late, cm, w, pv, ortho, projected, z_ref, a_ref, m_ref
):
    k = cm.shape[1]
    n = 3 * k

    def at(ref, i):
        return ref[i * k:(i + 1) * k]

    xw, xp, wp = at(mid, 1).T, at(early, 1), at(mid, 2)
    gram = jnp.concatenate([
        jnp.concatenate([at(early, 0), xw, xp], 1),
        jnp.concatenate([at(mid, 1), at(mid, 5), wp], 1),
        jnp.concatenate([xp.T, wp.T, at(early, 2)], 1)], 0) * inverse_rows
    inner = jnp.concatenate([
        jnp.concatenate([at(early, 3), at(late, 0), at(mid, 0)], 1),
        jnp.concatenate([at(mid, 3), at(late, 2), at(mid, 4)], 1),
        jnp.concatenate([at(early, 4), at(late, 1), at(early, 5)], 1)], 0) * inverse_rows
    below = lax.broadcasted_iota(jnp.int32, (n, n), 0)
    across = lax.broadcasted_iota(jnp.int32, (n, n), 1)
    on_diagonal = below == across
    eye = on_diagonal.astype(F32)
    weights = jnp.where(below < across, 1.0, jnp.where(on_diagonal, 0.5, 0.0))
    marked = gram * eye
    scale_row = lax.rsqrt(jnp.sum(marked, 0, keepdims=True))
    scale_column = lax.rsqrt(jnp.sum(marked, 1, keepdims=True))
    a_ref[...] = gram * scale_row * scale_column

    def error(z, split):
        a = a_ref[...]
        if split:
            return dot3(z, dot3(a, z), dot_t) - eye
        z = z.astype(BF16)
        return dot_t(z, dot(a.astype(BF16), z).astype(BF16)) - eye

    z_ref[...] = eye - (a_ref[...] - eye) * weights
    for _ in range(2):
        z = z_ref[...]
        move = error(z, False) * weights
        z_ref[...] = z - dot(z.astype(BF16), move.astype(BF16))

    def going(state):
        return jnp.logical_and(state[0] < 8, jnp.logical_not(state[1] < 2e-4))

    def step(state):
        z = z_ref[...]
        now = error(z, True)
        z_ref[...] = z - dot3(z, now * weights)
        return state[0] + 1, jnp.max(jnp.abs(now))

    _, left = lax.while_loop(going, step, (jnp.int32(0), jnp.float32(1.0)))
    lowest = jnp.min(jnp.where(on_diagonal, z_ref[...], 1.0))
    good = jnp.logical_and(left < 2e-4, lowest > 0.0)

    @pl.when(jnp.logical_not(good))
    def _():
        m_ref[...] = eye
        rows_at = lax.broadcasted_iota(jnp.int32, (n, 1), 0)

        def column(j, carry):
            row_a, row_m = a_ref[pl.ds(j, 1), :], m_ref[pl.ds(j, 1), :]
            a = a_ref[...]
            cut = jnp.sum(jnp.where(across == j, a, 0.0), 1, keepdims=True)
            pivot = jnp.sum(jnp.where(rows_at == j, cut, 0.0), 0, keepdims=True)
            factor = lax.rsqrt(pivot)
            row_a, row_m, cut = row_a * factor, row_m * factor, jnp.where(rows_at > j, cut * factor, 0.0)
            a_ref[...] = a - cut * row_a
            m_ref[...] = m_ref[...] - cut * row_m
            m_ref[pl.ds(j, 1), :] = row_m
            return carry

        lax.fori_loop(0, n, column, 0)
        z_ref[...] = m_ref[...].T

    inverse = z_ref[...] * scale_column
    high, low = halves(inverse)
    stacked = jnp.concatenate([cm[...], w[...], pv[...]], 1)
    s_high, s_low = halves(stacked)
    ortho[...] = dot(s_high, high) + (dot(s_high, low) + dot(s_low, high))
    half = dot3(inner, inverse)
    projected[...] = dot3(inverse, half, dot_t)


def vmem(count):
    return [pl.BlockSpec(memory_space=pltpu.VMEM)] * count


def on_device(
    current_modes, previous, diag_tiles, lateral_tiles, lateral_index, vertical_tiles, vertical_index, smoother
):
    tiers, rows = lax.axis_size("tier"), lax.axis_size("row")
    count = tiers * rows
    height, k = current_modes.shape
    bt = diag_tiles.shape[-1]
    cuts = []
    for total in (6 * k, 6 * k, 3 * k):
        chunk = 8
        while chunk * count < total or total % chunk:
            chunk += 8
        cuts.append((chunk, total // chunk))
    smem = pl.BlockSpec(memory_space=pltpu.SMEM)
    one = pl.BlockSpec(memory_space=pltpu.VMEM)
    pair = pltpu.VMEM((height, 2 * k), BF16)
    single = pltpu.VMEM((height, k), BF16)
    tall = pltpu.VMEM((height, bt), BF16)
    square = pltpu.VMEM((height, height), BF16)
    wide = pltpu.VMEM((height, 2 * k), F32)
    w, early, mid, late = pl.pallas_call(
        functools.partial(step_kernel, tiers, rows, cuts),
        out_shape=[
            jax.ShapeDtypeStruct((height, k), F32), jax.ShapeDtypeStruct((6 * k, k), F32),
            jax.ShapeDtypeStruct((6 * k, k), F32), jax.ShapeDtypeStruct((3 * k, k), F32)],
        in_specs=[one, one, one, one, smem, one, smem, one],
        out_specs=vmem(4),
        scratch_shapes=[
            pair, pair, pair, pair, pair,
            tall, tall, square, tall, tall, square,
            wide, wide, single, single, single, single, single,
            pltpu.VMEM((count, 8, k), F32),
            pltpu.VMEM((6 * k, k), F32), pltpu.VMEM((6 * k, k), F32), pltpu.VMEM((3 * k, k), F32),
        ] + [pltpu.VMEM((count, chunk, k), F32) for chunk, _ in cuts] + [
            pltpu.SemaphoreType.DMA((SEMS,)), pltpu.SemaphoreType.DMA((SEMS,))],
        compiler_params=pltpu.CompilerParams(
            collective_id=0, has_side_effects=True, vmem_limit_bytes=40 * 2**20),
        name="step",
    )(
        current_modes, previous, diag_tiles[0, 0], lateral_tiles[0, 0], lateral_index[0, 0],
        vertical_tiles[0, 0], vertical_index[0, 0], smoother[0, 0])
    n = 3 * k
    full = pltpu.VMEM((n, n), F32)
    return pl.pallas_call(
        functools.partial(basis_kernel, 1.0 / (height * count)),
        out_shape=[jax.ShapeDtypeStruct((height, n), F32), jax.ShapeDtypeStruct((n, n), F32)],
        in_specs=vmem(6),
        out_specs=vmem(2),
        scratch_shapes=[full, full, full],
        compiler_params=pltpu.CompilerParams(vmem_limit_bytes=40 * 2**20),
        name="basis",
    )(early, mid, late, current_modes, w, previous)


def solution(mesh):
    placed = (
        P(("tier", "row"), None),
        P(("tier", "row"), None),
        P("tier", "row", None, None, None),
        P("tier", "row", None, None, None, None),
        P("tier", "row", None, None),
        P("tier", "row", None, None, None),
        P("tier", "row", None),
        P("tier", "row", None, None, None),
    )
    return jax.shard_map(
        on_device,
        mesh=mesh,
        in_specs=placed,
        out_specs=(P(("tier", "row"), None), P()),
        check_vma=False,
    )
```

```python
import functools

import jax
import jax.numpy as jnp
from jax import lax
from jax.experimental import pallas as pl
from jax.experimental.pallas import tpu as pltpu
from jax.sharding import PartitionSpec as P

F32 = jnp.float32
BF16 = jnp.bfloat16
MESH = pl.DeviceIdType.MESH


def dot(a, b):
    return jnp.dot(a, b, preferred_element_type=F32)


def dot_t(a, b):
    return lax.dot_general(a, b, (((0,), (0,)), ((), ())), preferred_element_type=F32)


def halves(x):
    high = x.astype(BF16)
    return high, (x - high.astype(F32)).astype(BF16)


def dot3(a, b, product=dot):
    (a_high, a_low), (b_high, b_low) = halves(a), halves(b)
    return product(a_high, b_high) + (product(a_high, b_low) + product(a_low, b_high))


def flag(condition):
    return jnp.where(condition, 1.0, 0.0).astype(F32)


def scaled(tile, factor):
    return (tile.astype(F32) * factor).astype(BF16)


F_PREV, F_NEXT, F_LOW, F_UP, T_PREV, T_NEXT, T_LOW, P_UP, W_PREV, W_NEXT, W_LOW, W_UP, QUOT, X_UP = range(14)
SUM_AT = 14
SEMS = SUM_AT + 18


def step_kernel(
    tiers, rows,
    cm, pv, diag, lat, lat_at, vert, vert_at, smo,
    w_out, early, mid, late,
    f_own, f_prev, f_next, f_low, f_up,
    t_prev, t_next, t_low, got_prev, got_next, got_up,
    p_own, p_low, x_own, x_low, wb, wb_prev, wb_next, wb_low, wb_up,
    q_buf, src0, src1, src2, send_sem, recv_sem, *boxes,
):
    tier, row = lax.axis_index("tier"), lax.axis_index("row")
    count = tiers * rows
    me = tier * rows + row
    bt = diag.shape[-1]
    k = cm.shape[1]

    def place(d):
        return (lax.div(d, rows), lax.rem(d, rows))

    def others(body):
        def step(i, carry):
            body(lax.rem(me + i, count))
            return carry
        lax.fori_loop(1, count, step, 0)

    barrier = pltpu.get_barrier_semaphore()
    others(lambda d: pl.semaphore_signal(barrier, inc=1, device_id=place(d), device_id_type=MESH))

    def remote(src, dst, slot, device):
        return pltpu.make_async_remote_copy(
            src_ref=src, dst_ref=dst, send_sem=send_sem.at[slot], recv_sem=recv_sem.at[slot],
            device_id=device, device_id_type=MESH)

    has_prev, has_next = row > 0, row < rows - 1
    has_low, has_up = tier > 0, tier < tiers - 1
    PREV, NEXT = (has_prev, has_next, (tier, row - 1)), (has_next, has_prev, (tier, row + 1))
    LOW, UP = (has_low, has_up, (tier - 1, row)), (has_up, has_low, (tier + 1, row))

    def send(src, dst, slot, way):
        @pl.when(way[0])
        def _():
            remote(src, dst, slot, way[2]).start()

    def receive(src, dst, slot, way):
        @pl.when(way[1])
        def _():
            remote(src, dst, slot, (tier, row)).wait_recv()

    def sent(src, dst, slot, way):
        @pl.when(way[0])
        def _():
            remote(src, dst, slot, (tier, row)).wait_send()

    f_own[:, :k] = cm[...].astype(BF16)
    f_own[:, k:] = pv[...].astype(BF16)
    below = flag(lat_at[1, 0] == 0)
    inner_low = 1.0 - below
    above = flag(lat_at[0, 1] == 3)
    inner_up = 1.0 - above
    t_prev[:bt] = lat[0, 0]
    t_prev[bt:] = scaled(lat[1, 0], below)
    t_next[:bt] = scaled(lat[0, 1], above)
    t_next[bt:] = lat[1, 1]
    for g in range(2):
        swap = flag(vert_at[g] == 1)
        t_low[g * bt:(g + 1) * bt, :bt] = scaled(vert[g], 1.0 - swap)
        t_low[g * bt:(g + 1) * bt, bt:] = scaled(vert[g], swap)

    @pl.when(jnp.logical_not(has_prev))
    def _():
        f_prev[...] = jnp.zeros_like(f_prev)
        wb_prev[...] = jnp.zeros_like(wb_prev)
        got_prev[...] = jnp.zeros_like(got_prev)

    @pl.when(jnp.logical_not(has_next))
    def _():
        f_next[...] = jnp.zeros_like(f_next)
        wb_next[...] = jnp.zeros_like(wb_next)
        got_next[...] = jnp.zeros_like(got_next)

    @pl.when(jnp.logical_not(has_low))
    def _():
        f_low[...] = jnp.zeros_like(f_low)
        wb_low[...] = jnp.zeros_like(wb_low)
        p_low[...] = jnp.zeros_like(p_low)
        x_low[...] = jnp.zeros_like(x_low)

    @pl.when(jnp.logical_not(has_up))
    def _():
        f_up[...] = jnp.zeros_like(f_up)
        wb_up[...] = jnp.zeros_like(wb_up)
        got_up[...] = jnp.zeros_like(got_up)

    first = [
        (f_own, f_up, F_LOW, LOW), (f_own, f_low, F_UP, UP),
        (f_own, f_next, F_PREV, PREV), (f_own, f_prev, F_NEXT, NEXT),
        (t_low, got_up, T_LOW, LOW), (t_prev, got_next, T_PREV, PREV), (t_next, got_prev, T_NEXT, NEXT),
    ]
    second = [
        (wb, wb_up, W_LOW, LOW), (wb, wb_low, W_UP, UP),
        (wb, wb_next, W_PREV, PREV), (wb, wb_prev, W_NEXT, NEXT),
    ]
    pl.semaphore_wait(barrier, count - 1)
    for item in first:
        send(*item)

    zero = jnp.zeros((bt, bt), BF16)
    cross_up, cross_low = scaled(lat[0, 1], inner_up), scaled(lat[1, 0], inner_low)
    inner = jnp.concatenate([
        jnp.concatenate([diag[0], cross_up], 1), jnp.concatenate([cross_low, diag[1]], 1)], 0)
    crossed = jnp.concatenate([
        jnp.concatenate([zero, cross_up], 1), jnp.concatenate([cross_low, zero], 1)], 0)

    def local(own):
        return dot(inner, own) + dot_t(crossed, own)

    def coupled(total, prev, after, low, up):
        total = total + dot(t_prev[...], prev[bt:]) + dot(t_next[...], after[:bt])
        total = total + dot(t_low[...], low[...]) + dot_t(got_up[...], up[...])
        edge = jnp.concatenate([dot_t(got_prev[...], prev[...]), dot_t(got_next[...], after[...])], 0)
        return total + edge

    half_at = lax.rem(row, 2)
    plane_at = tier * 2 + lax.rem(lax.div(row, 2), 2)
    line_at = lax.div(row, 4)
    planes, lines = 2 * tiers, rows // 4
    buddy = (tier, row + 1 - 2 * half_at)

    def plane_place(j):
        return (lax.div(j, 2), line_at * 4 + lax.rem(j, 2) * 2 + half_at)

    def line_place(j):
        return (tier, j * 4 + lax.rem(row, 4))

    def around(size, own, body):
        def step(i, carry):
            body(lax.rem(own + i, size))
            return carry
        lax.fori_loop(1, size, step, 0)

    def arrived(part, slot):
        remote(part, part, slot, (tier, row)).wait_recv()

    def left(part, slot):
        remote(part, part, slot, (tier, row)).wait_send()

    class Sum:
        def __init__(self, which, src, part1, part2, box1, box2, box3, out):
            self.src, self.part1, self.part2, self.out = src, part1, part2, out
            self.box1, self.box2, self.box3 = box1, box2, box3
            self.slot = SUM_AT + 6 * which
            self.n1 = src.shape[0] // 2
            self.n2 = self.n1 // planes
            self.n3 = self.n2 // lines
            self.at1 = pl.multiple_of(half_at * self.n1, 8)
            self.at2 = pl.multiple_of(self.at1 + plane_at * self.n2, 8)
            self.at3 = pl.multiple_of(self.at2 + line_at * self.n3, 8)

        def send1(self):
            away = pl.multiple_of((1 - half_at) * self.n1, 8)
            remote(self.src.at[pl.ds(away, self.n1)], self.box1, self.slot, buddy).start()

        def send2(self):
            arrived(self.box1, self.slot)
            self.part1[...] = self.src[pl.ds(self.at1, self.n1)] + self.box1[...]
            def body(j):
                piece = self.part1.at[pl.ds(pl.multiple_of(j * self.n2, 8), self.n2)]
                remote(piece, self.box2.at[plane_at], self.slot + 1, plane_place(j)).start()
            around(planes, plane_at, body)
            mine = self.part1[pl.ds(pl.multiple_of(plane_at * self.n2, 8), self.n2)]
            self.box2[pl.ds(plane_at, 1)] = mine[None]

        def send3(self):
            arrived(self.box2.at[pl.ds(0, planes - 1)], self.slot + 1)
            self.part2[...] = jnp.sum(self.box2[...], axis=0)
            def body(j):
                piece = self.part2.at[pl.ds(pl.multiple_of(j * self.n3, 8), self.n3)]
                remote(piece, self.box3.at[line_at], self.slot + 2, line_place(j)).start()
            around(lines, line_at, body)
            mine = self.part2[pl.ds(pl.multiple_of(line_at * self.n3, 8), self.n3)]
            self.box3[pl.ds(line_at, 1)] = mine[None]

        def share3(self):
            arrived(self.box3.at[pl.ds(0, lines - 1)], self.slot + 2)
            part = self.out.at[pl.ds(self.at3, self.n3)]
            self.out[pl.ds(self.at3, self.n3)] = jnp.sum(self.box3[...], axis=0)
            around(lines, line_at, lambda j: remote(part, part, self.slot + 3, line_place(j)).start())

        def share2(self):
            arrived(self.out.at[pl.ds(0, self.n2 - self.n3)], self.slot + 3)
            part = self.out.at[pl.ds(self.at2, self.n2)]
            around(planes, plane_at, lambda j: remote(part, part, self.slot + 4, plane_place(j)).start())

        def share1(self):
            arrived(self.out.at[pl.ds(0, self.n1 - self.n2)], self.slot + 4)
            part = self.out.at[pl.ds(self.at1, self.n1)]
            remote(part, part, self.slot + 5, buddy).start()

        def end(self):
            whole = self.out.at[pl.ds(0, self.n1)]
            arrived(whole, self.slot + 5)
            left(whole, self.slot + 5)
            left(self.out.at[pl.ds(0, self.n1 - self.n2)], self.slot + 4)
            left(self.out.at[pl.ds(0, self.n2 - self.n3)], self.slot + 3)
            left(self.box3.at[pl.ds(0, lines - 1)], self.slot + 2)
            left(self.box2.at[pl.ds(0, planes - 1)], self.slot + 1)
            left(self.box1, self.slot)

    first_sum = Sum(0, src0, *boxes[0:5], early)
    second_sum = Sum(1, src1, *boxes[5:10], mid)
    third_sum = Sum(2, src2, *boxes[10:15], late)

    def smooth(field, low_ref, out):
        low_high, low_low = halves(low_ref[...])
        field = field - (dot(t_low[...], low_high) + dot(t_low[...], low_low))
        out[:bt] = dot3(smo[0], field[:bt])
        out[bt:] = dot3(smo[1], field[bt:])

    @pl.when(jnp.logical_not(has_low))
    def _():
        smooth(cm[...], x_low, x_own)
    @pl.when(jnp.logical_and(jnp.logical_not(has_low), has_up))
    def _():
        remote(x_own, x_low, X_UP, UP[2]).start()

    total = local(f_own[...])
    for item in first:
        receive(*item)
    image = coupled(total, f_prev, f_next, f_low, f_up)
    x, mode_image = cm[...], image[:, :k]
    q_buf[pl.ds(me, 1), 0:1] = jnp.sum(x * mode_image, 0, keepdims=True)[None]
    q_buf[pl.ds(me, 1), 1:2] = jnp.sum(x * x, 0, keepdims=True)[None]
    others(lambda d: remote(q_buf.at[me], q_buf.at[me], QUOT, place(d)).start())

    @pl.when(has_low)
    def _():
        arrived(x_low, X_UP)
        smooth(cm[...], x_low, x_own)
    @pl.when(jnp.logical_and(has_low, has_up))
    def _():
        remote(x_own, x_low, X_UP, UP[2]).start()
    receive(p_own, p_low, P_UP, UP)
    smooth(mode_image, p_low, p_own)
    send(p_own, p_low, P_UP, UP)

    fields = jnp.concatenate([x, pv[...]], 1)
    given = jnp.concatenate([fields, image], 1)
    product = dot3(fields, given, dot_t)
    src0[0 * k:1 * k] = product[:k, :k]
    src0[1 * k:2 * k] = product[:k, k:2 * k]
    src0[2 * k:3 * k] = product[k:, k:2 * k]
    src0[3 * k:4 * k] = product[:k, 2 * k:3 * k]
    src0[4 * k:5 * k] = product[k:, 2 * k:3 * k]
    src0[5 * k:6 * k] = product[k:, 3 * k:]
    src1[0 * k:1 * k] = product[:k, 3 * k:]
    first_sum.send1()

    everyone = q_buf.at[pl.ds(0, count - 1)]
    remote(everyone, everyone, QUOT, (tier, row)).wait_recv()
    sums = jnp.sum(q_buf[...], axis=0)
    w = p_own[...] - x_own[...] * (sums[0:1] / sums[1:2])
    w_out[...] = w
    wb[...] = w.astype(BF16)
    for item in second:
        send(*item)

    product = dot3(w, jnp.concatenate([given, w], 1), dot_t)
    for at in range(5):
        src1[(at + 1) * k:(at + 2) * k] = product[:, at * k:(at + 1) * k]
    second_sum.send1()
    first_sum.send2()
    total = local(wb[...])
    for item in second:
        receive(*item)
    work_image = coupled(total, wb_prev, wb_next, wb_low, wb_up)
    product = dot3(jnp.concatenate([fields, w], 1), work_image, dot_t)
    src2[:3 * k] = product
    third_sum.send1()
    second_sum.send2()
    first_sum.send3()
    third_sum.send2()
    second_sum.send3()
    first_sum.share3()
    third_sum.send3()
    second_sum.share3()
    first_sum.share2()
    third_sum.share3()
    second_sum.share2()
    first_sum.share1()
    third_sum.share2()
    second_sum.share1()
    third_sum.share1()
    first_sum.end()
    second_sum.end()
    third_sum.end()
    remote(everyone, everyone, QUOT, (tier, row)).wait_send()
    for item in first + second:
        sent(*item)
    sent(p_own, p_low, P_UP, UP)
    sent(x_own, x_low, X_UP, UP)


def basis_kernel(
    inverse_rows, early, mid, late, cm, w, pv, ortho, projected, z_ref, a_ref, m_ref
):
    k = cm.shape[1]
    n = 3 * k

    def at(ref, i):
        return ref[i * k:(i + 1) * k]

    xw, xp, wp = at(mid, 1).T, at(early, 1), at(mid, 2)
    gram = jnp.concatenate([
        jnp.concatenate([at(early, 0), xw, xp], 1),
        jnp.concatenate([at(mid, 1), at(mid, 5), wp], 1),
        jnp.concatenate([xp.T, wp.T, at(early, 2)], 1)], 0) * inverse_rows
    inner = jnp.concatenate([
        jnp.concatenate([at(early, 3), at(late, 0), at(mid, 0)], 1),
        jnp.concatenate([at(mid, 3), at(late, 2), at(mid, 4)], 1),
        jnp.concatenate([at(early, 4), at(late, 1), at(early, 5)], 1)], 0) * inverse_rows
    below = lax.broadcasted_iota(jnp.int32, (n, n), 0)
    across = lax.broadcasted_iota(jnp.int32, (n, n), 1)
    on_diagonal = below == across
    eye = on_diagonal.astype(F32)
    weights = jnp.where(below < across, 1.0, jnp.where(on_diagonal, 0.5, 0.0))
    marked = gram * eye
    scale_row = lax.rsqrt(jnp.sum(marked, 0, keepdims=True))
    scale_column = lax.rsqrt(jnp.sum(marked, 1, keepdims=True))
    a_ref[...] = gram * scale_row * scale_column

    def error(z, split):
        a = a_ref[...]
        if split:
            return dot3(z, dot3(a, z), dot_t) - eye
        z = z.astype(BF16)
        return dot_t(z, dot(a.astype(BF16), z).astype(BF16)) - eye

    z_ref[...] = eye - (a_ref[...] - eye) * weights
    for _ in range(2):
        z = z_ref[...]
        move = error(z, False) * weights
        z_ref[...] = z - dot(z.astype(BF16), move.astype(BF16))

    def going(state):
        return jnp.logical_and(state[0] < 8, jnp.logical_not(state[1] < 2e-4))

    def step(state):
        z = z_ref[...]
        now = error(z, True)
        z_ref[...] = z - dot3(z, now * weights)
        return state[0] + 1, jnp.max(jnp.abs(now))

    _, left = lax.while_loop(going, step, (jnp.int32(0), jnp.float32(1.0)))
    lowest = jnp.min(jnp.where(on_diagonal, z_ref[...], 1.0))
    good = jnp.logical_and(left < 2e-4, lowest > 0.0)

    @pl.when(jnp.logical_not(good))
    def _():
        m_ref[...] = eye
        rows_at = lax.broadcasted_iota(jnp.int32, (n, 1), 0)

        def column(j, carry):
            row_a, row_m = a_ref[pl.ds(j, 1), :], m_ref[pl.ds(j, 1), :]
            a = a_ref[...]
            cut = jnp.sum(jnp.where(across == j, a, 0.0), 1, keepdims=True)
            pivot = jnp.sum(jnp.where(rows_at == j, cut, 0.0), 0, keepdims=True)
            factor = lax.rsqrt(pivot)
            row_a, row_m, cut = row_a * factor, row_m * factor, jnp.where(rows_at > j, cut * factor, 0.0)
            a_ref[...] = a - cut * row_a
            m_ref[...] = m_ref[...] - cut * row_m
            m_ref[pl.ds(j, 1), :] = row_m
            return carry

        lax.fori_loop(0, n, column, 0)
        z_ref[...] = m_ref[...].T

    inverse = z_ref[...] * scale_column
    high, low = halves(inverse)
    stacked = jnp.concatenate([cm[...], w[...], pv[...]], 1)
    s_high, s_low = halves(stacked)
    ortho[...] = dot(s_high, high) + (dot(s_high, low) + dot(s_low, high))
    half = dot3(inner, inverse)
    projected[...] = dot3(inverse, half, dot_t)


def vmem(count):
    return [pl.BlockSpec(memory_space=pltpu.VMEM)] * count


def on_device(
    current_modes, previous, diag_tiles, lateral_tiles, lateral_index, vertical_tiles, vertical_index, smoother
):
    tiers, rows = lax.axis_size("tier"), lax.axis_size("row")
    count = tiers * rows
    height, k = current_modes.shape
    bt = diag_tiles.shape[-1]
    unit = 8 * count
    totals = [-(-blocks * k // unit) * unit for blocks in (6, 6, 3)]
    boxes = []
    for total in totals:
        n1 = total // 2
        n2 = n1 // (2 * tiers)
        n3 = n2 // (rows // 4)
        for shape in ((n1, k), (n2, k), (n1, k), (2 * tiers, n2, k), (rows // 4, n3, k)):
            boxes.append(pltpu.VMEM(shape, F32))
    smem = pl.BlockSpec(memory_space=pltpu.SMEM)
    one = pl.BlockSpec(memory_space=pltpu.VMEM)
    pair = pltpu.VMEM((height, 2 * k), BF16)
    single = pltpu.VMEM((height, k), BF16)
    tall = pltpu.VMEM((height, bt), BF16)
    square = pltpu.VMEM((height, height), BF16)
    wide = pltpu.VMEM((height, k), F32)
    w, early, mid, late = pl.pallas_call(
        functools.partial(step_kernel, tiers, rows),
        out_shape=[
            jax.ShapeDtypeStruct((height, k), F32)] + [
            jax.ShapeDtypeStruct((total, k), F32) for total in totals],
        in_specs=[one, one, one, one, smem, one, smem, one],
        out_specs=vmem(4),
        scratch_shapes=[
            pair, pair, pair, pair, pair,
            tall, tall, square, tall, tall, square,
            wide, wide, wide, wide, single, single, single, single, single,
            pltpu.VMEM((count, 8, k), F32),
        ] + [pltpu.VMEM((total, k), F32) for total in totals] + [
            pltpu.SemaphoreType.DMA((SEMS,)), pltpu.SemaphoreType.DMA((SEMS,))] + boxes,
        compiler_params=pltpu.CompilerParams(
            collective_id=0, has_side_effects=True, vmem_limit_bytes=40 * 2**20),
        name="step",
    )(
        current_modes, previous, diag_tiles[0, 0], lateral_tiles[0, 0], lateral_index[0, 0],
        vertical_tiles[0, 0], vertical_index[0, 0], smoother[0, 0])
    n = 3 * k
    full = pltpu.VMEM((n, n), F32)
    return pl.pallas_call(
        functools.partial(basis_kernel, 1.0 / (height * count)),
        out_shape=[jax.ShapeDtypeStruct((height, n), F32), jax.ShapeDtypeStruct((n, n), F32)],
        in_specs=vmem(6),
        out_specs=vmem(2),
        scratch_shapes=[full, full, full],
        compiler_params=pltpu.CompilerParams(vmem_limit_bytes=40 * 2**20),
        name="basis",
    )(early, mid, late, current_modes, w, previous)


def solution(mesh):
    placed = (
        P(("tier", "row"), None),
        P(("tier", "row"), None),
        P("tier", "row", None, None, None),
        P("tier", "row", None, None, None, None),
        P("tier", "row", None, None),
        P("tier", "row", None, None, None),
        P("tier", "row", None),
        P("tier", "row", None, None, None),
    )
    return jax.shard_map(
        on_device,
        mesh=mesh,
        in_specs=placed,
        out_specs=(P(("tier", "row"), None), P()),
        check_vma=False,
    )
```

```python
import functools

import jax
import jax.numpy as jnp
from jax import lax
from jax.experimental import pallas as pl
from jax.experimental.pallas import tpu as pltpu
from jax.sharding import PartitionSpec as P

F32 = jnp.float32
BF16 = jnp.bfloat16
MESH = pl.DeviceIdType.MESH


def dot(a, b):
    return jnp.dot(a, b, preferred_element_type=F32)


def dot_t(a, b):
    return lax.dot_general(a, b, (((0,), (0,)), ((), ())), preferred_element_type=F32)


def halves(x):
    high = x.astype(BF16)
    return high, (x - high.astype(F32)).astype(BF16)


def dot3(a, b, product=dot):
    (a_high, a_low), (b_high, b_low) = halves(a), halves(b)
    return product(a_high, b_high) + (product(a_high, b_low) + product(a_low, b_high))


def flag(condition):
    return jnp.where(condition, 1.0, 0.0).astype(F32)


def scaled(tile, factor):
    return (tile.astype(F32) * factor).astype(BF16)


F_PREV, F_NEXT, F_LOW, F_UP, T_PREV, T_NEXT, T_LOW, P_UP, W_PREV, W_NEXT, W_LOW, W_UP, QUOT, X_UP = range(14)
SUM_AT = 14
SEMS = SUM_AT + 18


def step_kernel(
    tiers, rows,
    cm_in, pv_in, diag_in, lat_in, lat_at, vert_in, vert_at, smo_in,
    stacked, early, mid, late,
    diag, lat, vert, smo, load_sem,
    f_own, f_prev, f_next, f_low, f_up,
    t_prev, t_next, t_low, got_prev, got_next, got_up,
    p_own, p_low, x_own, x_low, wb, wb_prev, wb_next, wb_low, wb_up,
    q_buf, src0, src1, src2, send_sem, recv_sem, *boxes,
):
    tier, row = lax.axis_index("tier"), lax.axis_index("row")
    count = tiers * rows
    me = tier * rows + row
    bt = diag.shape[-1]
    k = cm_in.shape[1]
    cm, w_out, pv = [stacked.at[:, i * k:(i + 1) * k] for i in range(3)]
    loads = [
        pltpu.make_async_copy(source, target, load_sem.at[i]) for i, (source, target) in enumerate(
            [(cm_in, cm), (pv_in, pv), (lat_in, lat), (vert_in, vert), (diag_in, diag), (smo_in, smo)])]
    for load in loads:
        load.start()

    def place(d):
        return (lax.div(d, rows), lax.rem(d, rows))

    def others(body):
        def step(i, carry):
            body(lax.rem(me + i, count))
            return carry
        lax.fori_loop(1, count, step, 0)

    barrier = pltpu.get_barrier_semaphore()
    others(lambda d: pl.semaphore_signal(barrier, inc=1, device_id=place(d), device_id_type=MESH))

    def remote(src, dst, slot, device):
        return pltpu.make_async_remote_copy(
            src_ref=src, dst_ref=dst, send_sem=send_sem.at[slot], recv_sem=recv_sem.at[slot],
            device_id=device, device_id_type=MESH)

    has_prev, has_next = row > 0, row < rows - 1
    has_low, has_up = tier > 0, tier < tiers - 1
    PREV, NEXT = (has_prev, has_next, (tier, row - 1)), (has_next, has_prev, (tier, row + 1))
    LOW, UP = (has_low, has_up, (tier - 1, row)), (has_up, has_low, (tier + 1, row))

    def send(src, dst, slot, way):
        @pl.when(way[0])
        def _():
            remote(src, dst, slot, way[2]).start()

    def receive(src, dst, slot, way):
        @pl.when(way[1])
        def _():
            remote(src, dst, slot, (tier, row)).wait_recv()

    def sent(src, dst, slot, way):
        @pl.when(way[0])
        def _():
            remote(src, dst, slot, (tier, row)).wait_send()

    for load in loads:
        load.wait()
    f_own[:, :k] = cm[...].astype(BF16)
    f_own[:, k:] = pv[...].astype(BF16)
    below = flag(lat_at[1, 0] == 0)
    inner_low = 1.0 - below
    above = flag(lat_at[0, 1] == 3)
    inner_up = 1.0 - above
    t_prev[:bt] = lat[0, 0]
    t_prev[bt:] = scaled(lat[1, 0], below)
    t_next[:bt] = scaled(lat[0, 1], above)
    t_next[bt:] = lat[1, 1]
    for g in range(2):
        swap = flag(vert_at[g] == 1)
        t_low[g * bt:(g + 1) * bt, :bt] = scaled(vert[g], 1.0 - swap)
        t_low[g * bt:(g + 1) * bt, bt:] = scaled(vert[g], swap)

    @pl.when(jnp.logical_not(has_prev))
    def _():
        f_prev[...] = jnp.zeros_like(f_prev)
        wb_prev[...] = jnp.zeros_like(wb_prev)
        got_prev[...] = jnp.zeros_like(got_prev)

    @pl.when(jnp.logical_not(has_next))
    def _():
        f_next[...] = jnp.zeros_like(f_next)
        wb_next[...] = jnp.zeros_like(wb_next)
        got_next[...] = jnp.zeros_like(got_next)

    @pl.when(jnp.logical_not(has_low))
    def _():
        f_low[...] = jnp.zeros_like(f_low)
        wb_low[...] = jnp.zeros_like(wb_low)
        p_low[...] = jnp.zeros_like(p_low)
        x_low[...] = jnp.zeros_like(x_low)

    @pl.when(jnp.logical_not(has_up))
    def _():
        f_up[...] = jnp.zeros_like(f_up)
        wb_up[...] = jnp.zeros_like(wb_up)
        got_up[...] = jnp.zeros_like(got_up)

    first = [
        (f_own, f_up, F_LOW, LOW), (f_own, f_low, F_UP, UP),
        (f_own, f_next, F_PREV, PREV), (f_own, f_prev, F_NEXT, NEXT),
        (t_low, got_up, T_LOW, LOW), (t_prev, got_next, T_PREV, PREV), (t_next, got_prev, T_NEXT, NEXT),
    ]
    second = [
        (wb, wb_up, W_LOW, LOW), (wb, wb_low, W_UP, UP),
        (wb, wb_next, W_PREV, PREV), (wb, wb_prev, W_NEXT, NEXT),
    ]
    pl.semaphore_wait(barrier, count - 1)
    for item in first:
        send(*item)

    zero = jnp.zeros((bt, bt), BF16)
    cross_up, cross_low = scaled(lat[0, 1], inner_up), scaled(lat[1, 0], inner_low)
    inner = jnp.concatenate([
        jnp.concatenate([diag[0], cross_up], 1), jnp.concatenate([cross_low, diag[1]], 1)], 0)
    crossed = jnp.concatenate([
        jnp.concatenate([zero, cross_up], 1), jnp.concatenate([cross_low, zero], 1)], 0)

    def local(own):
        return dot(inner, own) + dot_t(crossed, own)

    def coupled(total, prev, after, low, up):
        total = total + dot(t_prev[...], prev[bt:]) + dot(t_next[...], after[:bt])
        total = total + dot(t_low[...], low[...]) + dot_t(got_up[...], up[...])
        edge = jnp.concatenate([dot_t(got_prev[...], prev[...]), dot_t(got_next[...], after[...])], 0)
        return total + edge

    half_at = lax.rem(row, 2)
    plane_at = tier * 2 + lax.rem(lax.div(row, 2), 2)
    line_at = lax.div(row, 4)
    planes, lines = 2 * tiers, rows // 4
    buddy = (tier, row + 1 - 2 * half_at)

    def plane_place(j):
        return (lax.div(j, 2), line_at * 4 + lax.rem(j, 2) * 2 + half_at)

    def line_place(j):
        return (tier, j * 4 + lax.rem(row, 4))

    def around(size, own, body):
        def step(i, carry):
            body(lax.rem(own + i, size))
            return carry
        lax.fori_loop(1, size, step, 0)

    def arrived(part, slot):
        remote(part, part, slot, (tier, row)).wait_recv()

    def left(part, slot):
        remote(part, part, slot, (tier, row)).wait_send()

    class Sum:
        def __init__(self, which, src, part1, part2, box1, box2, box3, out):
            self.src, self.part1, self.part2, self.out = src, part1, part2, out
            self.box1, self.box2, self.box3 = box1, box2, box3
            self.slot = SUM_AT + 6 * which
            self.n1 = src.shape[0] // 2
            self.n2 = self.n1 // planes
            self.n3 = self.n2 // lines
            self.at1 = pl.multiple_of(half_at * self.n1, 8)
            self.at2 = pl.multiple_of(self.at1 + plane_at * self.n2, 8)
            self.at3 = pl.multiple_of(self.at2 + line_at * self.n3, 8)

        def send1(self):
            away = pl.multiple_of((1 - half_at) * self.n1, 8)
            remote(self.src.at[pl.ds(away, self.n1)], self.box1, self.slot, buddy).start()

        def send2(self):
            arrived(self.box1, self.slot)
            self.part1[...] = self.src[pl.ds(self.at1, self.n1)] + self.box1[...]
            def body(j):
                piece = self.part1.at[pl.ds(pl.multiple_of(j * self.n2, 8), self.n2)]
                remote(piece, self.box2.at[plane_at], self.slot + 1, plane_place(j)).start()
            around(planes, plane_at, body)
            mine = self.part1[pl.ds(pl.multiple_of(plane_at * self.n2, 8), self.n2)]
            self.box2[pl.ds(plane_at, 1)] = mine[None]

        def send3(self):
            arrived(self.box2.at[pl.ds(0, planes - 1)], self.slot + 1)
            self.part2[...] = jnp.sum(self.box2[...], axis=0)
            def body(j):
                piece = self.part2.at[pl.ds(pl.multiple_of(j * self.n3, 8), self.n3)]
                remote(piece, self.box3.at[line_at], self.slot + 2, line_place(j)).start()
            around(lines, line_at, body)
            mine = self.part2[pl.ds(pl.multiple_of(line_at * self.n3, 8), self.n3)]
            self.box3[pl.ds(line_at, 1)] = mine[None]

        def share3(self):
            arrived(self.box3.at[pl.ds(0, lines - 1)], self.slot + 2)
            part = self.out.at[pl.ds(self.at3, self.n3)]
            self.out[pl.ds(self.at3, self.n3)] = jnp.sum(self.box3[...], axis=0)
            around(lines, line_at, lambda j: remote(part, part, self.slot + 3, line_place(j)).start())

        def share2(self):
            arrived(self.out.at[pl.ds(0, self.n2 - self.n3)], self.slot + 3)
            part = self.out.at[pl.ds(self.at2, self.n2)]
            around(planes, plane_at, lambda j: remote(part, part, self.slot + 4, plane_place(j)).start())

        def share1(self):
            arrived(self.out.at[pl.ds(0, self.n1 - self.n2)], self.slot + 4)
            part = self.out.at[pl.ds(self.at1, self.n1)]
            remote(part, part, self.slot + 5, buddy).start()

        def end(self):
            whole = self.out.at[pl.ds(0, self.n1)]
            arrived(whole, self.slot + 5)
            left(whole, self.slot + 5)
            left(self.out.at[pl.ds(0, self.n1 - self.n2)], self.slot + 4)
            left(self.out.at[pl.ds(0, self.n2 - self.n3)], self.slot + 3)
            left(self.box3.at[pl.ds(0, lines - 1)], self.slot + 2)
            left(self.box2.at[pl.ds(0, planes - 1)], self.slot + 1)
            left(self.box1, self.slot)

    first_sum = Sum(0, src0, *boxes[0:5], early)
    second_sum = Sum(1, src1, *boxes[5:10], mid)
    third_sum = Sum(2, src2, *boxes[10:15], late)

    def smooth(field, low_ref, out):
        low_high, low_low = halves(low_ref[...])
        field = field - (dot(t_low[...], low_high) + dot(t_low[...], low_low))
        out[:bt] = dot3(smo[0], field[:bt])
        out[bt:] = dot3(smo[1], field[bt:])

    @pl.when(jnp.logical_not(has_low))
    def _():
        smooth(cm[...], x_low, x_own)
    @pl.when(jnp.logical_and(jnp.logical_not(has_low), has_up))
    def _():
        remote(x_own, x_low, X_UP, UP[2]).start()

    total = local(f_own[...])
    for item in first:
        receive(*item)
    image = coupled(total, f_prev, f_next, f_low, f_up)
    x, mode_image = cm[...], image[:, :k]
    q_buf[pl.ds(me, 1), 0:1] = jnp.sum(x * mode_image, 0, keepdims=True)[None]
    q_buf[pl.ds(me, 1), 1:2] = jnp.sum(x * x, 0, keepdims=True)[None]
    others(lambda d: remote(q_buf.at[me], q_buf.at[me], QUOT, place(d)).start())

    @pl.when(has_low)
    def _():
        arrived(x_low, X_UP)
        smooth(cm[...], x_low, x_own)
    @pl.when(jnp.logical_and(has_low, has_up))
    def _():
        remote(x_own, x_low, X_UP, UP[2]).start()
    receive(p_own, p_low, P_UP, UP)
    smooth(mode_image, p_low, p_own)
    send(p_own, p_low, P_UP, UP)

    fields = jnp.concatenate([x, pv[...]], 1)
    given = jnp.concatenate([fields, image], 1)
    product = dot3(fields, given, dot_t)
    src0[0 * k:1 * k] = product[:k, :k]
    src0[1 * k:2 * k] = product[:k, k:2 * k]
    src0[2 * k:3 * k] = product[k:, k:2 * k]
    src0[3 * k:4 * k] = product[:k, 2 * k:3 * k]
    src0[4 * k:5 * k] = product[k:, 2 * k:3 * k]
    src0[5 * k:6 * k] = product[k:, 3 * k:]
    src1[0 * k:1 * k] = product[:k, 3 * k:]
    first_sum.send1()

    everyone = q_buf.at[pl.ds(0, count - 1)]
    remote(everyone, everyone, QUOT, (tier, row)).wait_recv()
    sums = jnp.sum(q_buf[...], axis=0)
    w = p_own[...] - x_own[...] * (sums[0:1] / sums[1:2])
    w_out[...] = w
    wb[...] = w.astype(BF16)
    for item in second:
        send(*item)

    product = dot3(w, jnp.concatenate([given, w], 1), dot_t)
    for at in range(5):
        src1[(at + 1) * k:(at + 2) * k] = product[:, at * k:(at + 1) * k]
    second_sum.send1()
    first_sum.send2()
    total = local(wb[...])
    for item in second:
        receive(*item)
    work_image = coupled(total, wb_prev, wb_next, wb_low, wb_up)
    product = dot3(jnp.concatenate([fields, w], 1), work_image, dot_t)
    src2[:3 * k] = product
    third_sum.send1()
    second_sum.send2()
    first_sum.send3()
    third_sum.send2()
    second_sum.send3()
    first_sum.share3()
    third_sum.send3()
    second_sum.share3()
    first_sum.share2()
    third_sum.share3()
    second_sum.share2()
    first_sum.share1()
    third_sum.share2()
    second_sum.share1()
    third_sum.share1()
    first_sum.end()
    second_sum.end()
    third_sum.end()
    remote(everyone, everyone, QUOT, (tier, row)).wait_send()
    for item in first + second:
        sent(*item)
    sent(p_own, p_low, P_UP, UP)
    sent(x_own, x_low, X_UP, UP)


def basis_kernel(
    inverse_rows, early, mid, late, stacked, ortho, projected, z_ref, a_ref, m_ref
):
    n = stacked.shape[1]
    k = n // 3

    def at(ref, i):
        return ref[i * k:(i + 1) * k]

    xw, xp, wp = at(mid, 1).T, at(early, 1), at(mid, 2)
    gram = jnp.concatenate([
        jnp.concatenate([at(early, 0), xw, xp], 1),
        jnp.concatenate([at(mid, 1), at(mid, 5), wp], 1),
        jnp.concatenate([xp.T, wp.T, at(early, 2)], 1)], 0) * inverse_rows
    inner = jnp.concatenate([
        jnp.concatenate([at(early, 3), at(late, 0), at(mid, 0)], 1),
        jnp.concatenate([at(mid, 3), at(late, 2), at(mid, 4)], 1),
        jnp.concatenate([at(early, 4), at(late, 1), at(early, 5)], 1)], 0) * inverse_rows
    below = lax.broadcasted_iota(jnp.int32, (n, n), 0)
    across = lax.broadcasted_iota(jnp.int32, (n, n), 1)
    on_diagonal = below == across
    eye = on_diagonal.astype(F32)
    weights = jnp.where(below < across, 1.0, jnp.where(on_diagonal, 0.5, 0.0))
    marked = gram * eye
    scale_row = lax.rsqrt(jnp.sum(marked, 0, keepdims=True))
    scale_column = lax.rsqrt(jnp.sum(marked, 1, keepdims=True))
    a_ref[...] = gram * scale_row * scale_column

    def error(z, split):
        a = a_ref[...]
        if split:
            return dot3(z, dot3(a, z), dot_t) - eye
        z = z.astype(BF16)
        return dot_t(z, dot(a.astype(BF16), z).astype(BF16)) - eye

    z_ref[...] = eye - (a_ref[...] - eye) * weights
    for _ in range(2):
        z = z_ref[...]
        move = error(z, False) * weights
        z_ref[...] = z - dot(z.astype(BF16), move.astype(BF16))

    def going(state):
        return jnp.logical_and(state[0] < 8, jnp.logical_not(state[1] < 2e-4))

    def step(state):
        z = z_ref[...]
        now = error(z, True)
        z_ref[...] = z - dot3(z, now * weights)
        return state[0] + 1, jnp.max(jnp.abs(now))

    _, left = lax.while_loop(going, step, (jnp.int32(0), jnp.float32(1.0)))
    lowest = jnp.min(jnp.where(on_diagonal, z_ref[...], 1.0))
    good = jnp.logical_and(left < 2e-4, lowest > 0.0)

    @pl.when(jnp.logical_not(good))
    def _():
        m_ref[...] = eye
        rows_at = lax.broadcasted_iota(jnp.int32, (n, 1), 0)

        def column(j, carry):
            row_a, row_m = a_ref[pl.ds(j, 1), :], m_ref[pl.ds(j, 1), :]
            a = a_ref[...]
            cut = jnp.sum(jnp.where(across == j, a, 0.0), 1, keepdims=True)
            pivot = jnp.sum(jnp.where(rows_at == j, cut, 0.0), 0, keepdims=True)
            factor = lax.rsqrt(pivot)
            row_a, row_m, cut = row_a * factor, row_m * factor, jnp.where(rows_at > j, cut * factor, 0.0)
            a_ref[...] = a - cut * row_a
            m_ref[...] = m_ref[...] - cut * row_m
            m_ref[pl.ds(j, 1), :] = row_m
            return carry

        lax.fori_loop(0, n, column, 0)
        z_ref[...] = m_ref[...].T

    inverse = z_ref[...] * scale_column
    high, low = halves(inverse)
    s_high, s_low = halves(stacked[...])
    ortho[...] = dot(s_high, high) + (dot(s_high, low) + dot(s_low, high))
    half = dot3(inner, inverse)
    projected[...] = dot3(inverse, half, dot_t)


def vmem(count):
    return [pl.BlockSpec(memory_space=pltpu.VMEM)] * count


def on_device(
    current_modes, previous, diag_tiles, lateral_tiles, lateral_index, vertical_tiles, vertical_index, smoother
):
    tiers, rows = lax.axis_size("tier"), lax.axis_size("row")
    count = tiers * rows
    height, k = current_modes.shape
    bt = diag_tiles.shape[-1]
    unit = 8 * count
    totals = [-(-blocks * k // unit) * unit for blocks in (6, 6, 3)]
    boxes = []
    for total in totals:
        n1 = total // 2
        n2 = n1 // (2 * tiers)
        n3 = n2 // (rows // 4)
        for shape in ((n1, k), (n2, k), (n1, k), (2 * tiers, n2, k), (rows // 4, n3, k)):
            boxes.append(pltpu.VMEM(shape, F32))
    smem = pl.BlockSpec(memory_space=pltpu.SMEM)
    hbm = pl.BlockSpec(memory_space=pltpu.HBM)
    pair = pltpu.VMEM((height, 2 * k), BF16)
    single = pltpu.VMEM((height, k), BF16)
    tall = pltpu.VMEM((height, bt), BF16)
    square = pltpu.VMEM((height, height), BF16)
    wide = pltpu.VMEM((height, k), F32)
    stacked, early, mid, late = pl.pallas_call(
        functools.partial(step_kernel, tiers, rows),
        out_shape=[
            jax.ShapeDtypeStruct((height, 3 * k), F32)] + [
            jax.ShapeDtypeStruct((total, k), F32) for total in totals],
        in_specs=[hbm, hbm, hbm, hbm, smem, hbm, smem, hbm],
        out_specs=vmem(4),
        scratch_shapes=[
            pltpu.VMEM((2, bt, bt), BF16), pltpu.VMEM((2, 2, bt, bt), BF16), pltpu.VMEM((2, bt, bt), BF16),
            pltpu.VMEM((2, bt, bt), F32), pltpu.SemaphoreType.DMA((6,)),
            pair, pair, pair, pair, pair,
            tall, tall, square, tall, tall, square,
            wide, wide, wide, wide, single, single, single, single, single,
            pltpu.VMEM((count, 8, k), F32),
        ] + [pltpu.VMEM((total, k), F32) for total in totals] + [
            pltpu.SemaphoreType.DMA((SEMS,)), pltpu.SemaphoreType.DMA((SEMS,))] + boxes,
        compiler_params=pltpu.CompilerParams(
            collective_id=0, has_side_effects=True, vmem_limit_bytes=60 * 2**20),
        name="step",
    )(
        current_modes, previous, diag_tiles[0, 0], lateral_tiles[0, 0], lateral_index[0, 0],
        vertical_tiles[0, 0], vertical_index[0, 0], smoother[0, 0])
    n = 3 * k
    full = pltpu.VMEM((n, n), F32)
    return pl.pallas_call(
        functools.partial(basis_kernel, 1.0 / (height * count)),
        out_shape=[jax.ShapeDtypeStruct((height, n), F32), jax.ShapeDtypeStruct((n, n), F32)],
        in_specs=vmem(4),
        out_specs=vmem(2),
        scratch_shapes=[full, full, full],
        compiler_params=pltpu.CompilerParams(vmem_limit_bytes=60 * 2**20),
        name="basis",
    )(early, mid, late, stacked)


def solution(mesh):
    placed = (
        P(("tier", "row"), None),
        P(("tier", "row"), None),
        P("tier", "row", None, None, None),
        P("tier", "row", None, None, None, None),
        P("tier", "row", None, None),
        P("tier", "row", None, None, None),
        P("tier", "row", None),
        P("tier", "row", None, None, None),
    )
    return jax.shard_map(
        on_device,
        mesh=mesh,
        in_specs=placed,
        out_specs=(P(("tier", "row"), None), P()),
        check_vma=False,
    )
```

```python
import functools

import jax
import jax.numpy as jnp
from jax import lax
from jax.experimental import pallas as pl
from jax.experimental.pallas import tpu as pltpu
from jax.sharding import PartitionSpec as P

F32 = jnp.float32
BF16 = jnp.bfloat16
MESH = pl.DeviceIdType.MESH


def dot(a, b):
    return jnp.dot(a, b, preferred_element_type=F32)


def dot_t(a, b):
    return lax.dot_general(a, b, (((0,), (0,)), ((), ())), preferred_element_type=F32)


def halves(x):
    high = x.astype(BF16)
    return high, (x - high.astype(F32)).astype(BF16)


def dot3(a, b, product=dot):
    (a_high, a_low), (b_high, b_low) = halves(a), halves(b)
    return product(a_high, b_high) + (product(a_high, b_low) + product(a_low, b_high))


def flag(condition):
    return jnp.where(condition, 1.0, 0.0).astype(F32)


def scaled(tile, factor):
    return (tile.astype(F32) * factor).astype(BF16)


F_PREV, F_NEXT, F_LOW, F_UP, T_PREV, T_NEXT, T_LOW, P_UP, W_PREV, W_NEXT, W_LOW, W_UP, QUOT, X_UP, FLAG_LOW = range(15)
SUM_AT = 15
SEMS = SUM_AT + 18


def step_kernel(
    tiers, rows,
    cm_in, pv_in, diag_in, lat_in, lat_at, vert_in, vert_at, smo_in,
    stacked, early, mid, late,
    diag, lat, vert, smo, load_sem, swaps, got_swaps, got_vert,
    f_own, f_prev, f_next, f_low, f_up,
    t_prev, t_next, t_low, got_prev, got_next, got_up,
    p_own, p_low, x_own, x_low, wb, wb_prev, wb_next, wb_low, wb_up,
    q_buf, src0, src1, src2, send_sem, recv_sem, *boxes,
):
    tier, row = lax.axis_index("tier"), lax.axis_index("row")
    count = tiers * rows
    me = tier * rows + row
    bt = diag.shape[-1]
    k = cm_in.shape[1]
    cm, w_out, pv = [stacked.at[:, i * k:(i + 1) * k] for i in range(3)]
    loads = [
        pltpu.make_async_copy(source, target, load_sem.at[i]) for i, (source, target) in enumerate(
            [(cm_in, cm), (pv_in, pv), (lat_in, lat), (vert_in, vert), (diag_in, diag), (smo_in, smo)])]
    for load in loads:
        load.start()

    def place(d):
        return (lax.div(d, rows), lax.rem(d, rows))

    def others(body):
        def step(i, carry):
            body(lax.rem(me + i, count))
            return carry
        lax.fori_loop(1, count, step, 0)

    barrier = pltpu.get_barrier_semaphore()
    others(lambda d: pl.semaphore_signal(barrier, inc=1, device_id=place(d), device_id_type=MESH))

    def remote(src, dst, slot, device):
        return pltpu.make_async_remote_copy(
            src_ref=src, dst_ref=dst, send_sem=send_sem.at[slot], recv_sem=recv_sem.at[slot],
            device_id=device, device_id_type=MESH)

    has_prev, has_next = row > 0, row < rows - 1
    has_low, has_up = tier > 0, tier < tiers - 1
    PREV, NEXT = (has_prev, has_next, (tier, row - 1)), (has_next, has_prev, (tier, row + 1))
    LOW, UP = (has_low, has_up, (tier - 1, row)), (has_up, has_low, (tier + 1, row))

    def send(src, dst, slot, way):
        @pl.when(way[0])
        def _():
            remote(src, dst, slot, way[2]).start()

    def receive(src, dst, slot, way):
        @pl.when(way[1])
        def _():
            remote(src, dst, slot, (tier, row)).wait_recv()

    def sent(src, dst, slot, way):
        @pl.when(way[0])
        def _():
            remote(src, dst, slot, (tier, row)).wait_send()

    for load in loads:
        load.wait()
    f_own[:, :k] = cm[...].astype(BF16)
    f_own[:, k:] = pv[...].astype(BF16)
    below = flag(lat_at[1, 0] == 0)
    inner_low = 1.0 - below
    above = flag(lat_at[0, 1] == 3)
    inner_up = 1.0 - above
    t_prev[:bt] = lat[0, 0]
    t_prev[bt:] = scaled(lat[1, 0], below)
    t_next[:bt] = scaled(lat[0, 1], above)
    t_next[bt:] = lat[1, 1]
    for g in range(2):
        swap = flag(vert_at[g] == 1)
        swaps[g * 16:(g + 1) * 16] = scaled(jnp.ones((16, bt), BF16), swap)
        t_low[g * bt:(g + 1) * bt, :bt] = scaled(vert[g], 1.0 - swap)
        t_low[g * bt:(g + 1) * bt, bt:] = scaled(vert[g], swap)

    @pl.when(jnp.logical_not(has_prev))
    def _():
        f_prev[...] = jnp.zeros_like(f_prev)
        wb_prev[...] = jnp.zeros_like(wb_prev)
        got_prev[...] = jnp.zeros_like(got_prev)

    @pl.when(jnp.logical_not(has_next))
    def _():
        f_next[...] = jnp.zeros_like(f_next)
        wb_next[...] = jnp.zeros_like(wb_next)
        got_next[...] = jnp.zeros_like(got_next)

    @pl.when(jnp.logical_not(has_low))
    def _():
        f_low[...] = jnp.zeros_like(f_low)
        wb_low[...] = jnp.zeros_like(wb_low)
        p_low[...] = jnp.zeros_like(p_low)
        x_low[...] = jnp.zeros_like(x_low)

    @pl.when(jnp.logical_not(has_up))
    def _():
        f_up[...] = jnp.zeros_like(f_up)
        wb_up[...] = jnp.zeros_like(wb_up)
        got_up[...] = jnp.zeros_like(got_up)

    first = [
        (f_own, f_up, F_LOW, LOW), (f_own, f_low, F_UP, UP),
        (f_own, f_next, F_PREV, PREV), (f_own, f_prev, F_NEXT, NEXT),
        (vert, got_vert, T_LOW, LOW), (swaps, got_swaps, FLAG_LOW, LOW), (t_prev, got_next, T_PREV, PREV), (t_next, got_prev, T_NEXT, NEXT),
    ]
    second = [
        (wb, wb_up, W_LOW, LOW), (wb, wb_low, W_UP, UP),
        (wb, wb_next, W_PREV, PREV), (wb, wb_prev, W_NEXT, NEXT),
    ]
    pl.semaphore_wait(barrier, count - 1)
    for item in first:
        send(*item)

    zero = jnp.zeros((bt, bt), BF16)
    cross_up, cross_low = scaled(lat[0, 1], inner_up), scaled(lat[1, 0], inner_low)
    inner = jnp.concatenate([
        jnp.concatenate([diag[0], cross_up], 1), jnp.concatenate([cross_low, diag[1]], 1)], 0)
    crossed = jnp.concatenate([
        jnp.concatenate([zero, cross_up], 1), jnp.concatenate([cross_low, zero], 1)], 0)

    def local(own):
        return dot(inner, own) + dot_t(crossed, own)

    def coupled(total, prev, after, low, up):
        total = total + dot(t_prev[...], prev[bt:]) + dot(t_next[...], after[:bt])
        total = total + dot(t_low[...], low[...]) + dot_t(got_up[...], up[...])
        edge = jnp.concatenate([dot_t(got_prev[...], prev[...]), dot_t(got_next[...], after[...])], 0)
        return total + edge

    half_at = lax.rem(row, 2)
    plane_at = tier * 2 + lax.rem(lax.div(row, 2), 2)
    line_at = lax.div(row, 4)
    planes, lines = 2 * tiers, rows // 4
    buddy = (tier, row + 1 - 2 * half_at)

    def plane_place(j):
        return (lax.div(j, 2), line_at * 4 + lax.rem(j, 2) * 2 + half_at)

    def line_place(j):
        return (tier, j * 4 + lax.rem(row, 4))

    def around(size, own, body):
        def step(i, carry):
            body(lax.rem(own + i, size))
            return carry
        lax.fori_loop(1, size, step, 0)

    def arrived(part, slot):
        remote(part, part, slot, (tier, row)).wait_recv()

    def left(part, slot):
        remote(part, part, slot, (tier, row)).wait_send()

    class Sum:
        def __init__(self, which, src, part1, part2, box1, box2, box3, out):
            self.src, self.part1, self.part2, self.out = src, part1, part2, out
            self.box1, self.box2, self.box3 = box1, box2, box3
            self.slot = SUM_AT + 6 * which
            self.n1 = src.shape[0] // 2
            self.n2 = self.n1 // planes
            self.n3 = self.n2 // lines
            self.at1 = pl.multiple_of(half_at * self.n1, 8)
            self.at2 = pl.multiple_of(self.at1 + plane_at * self.n2, 8)
            self.at3 = pl.multiple_of(self.at2 + line_at * self.n3, 8)

        def send1(self):
            away = pl.multiple_of((1 - half_at) * self.n1, 8)
            remote(self.src.at[pl.ds(away, self.n1)], self.box1, self.slot, buddy).start()

        def send2(self):
            arrived(self.box1, self.slot)
            self.part1[...] = self.src[pl.ds(self.at1, self.n1)] + self.box1[...]
            def body(j):
                piece = self.part1.at[pl.ds(pl.multiple_of(j * self.n2, 8), self.n2)]
                remote(piece, self.box2.at[plane_at], self.slot + 1, plane_place(j)).start()
            around(planes, plane_at, body)
            mine = self.part1[pl.ds(pl.multiple_of(plane_at * self.n2, 8), self.n2)]
            self.box2[pl.ds(plane_at, 1)] = mine[None]

        def send3(self):
            arrived(self.box2.at[pl.ds(0, planes - 1)], self.slot + 1)
            self.part2[...] = jnp.sum(self.box2[...], axis=0)
            def body(j):
                piece = self.part2.at[pl.ds(pl.multiple_of(j * self.n3, 8), self.n3)]
                remote(piece, self.box3.at[line_at], self.slot + 2, line_place(j)).start()
            around(lines, line_at, body)
            mine = self.part2[pl.ds(pl.multiple_of(line_at * self.n3, 8), self.n3)]
            self.box3[pl.ds(line_at, 1)] = mine[None]

        def share3(self):
            arrived(self.box3.at[pl.ds(0, lines - 1)], self.slot + 2)
            part = self.out.at[pl.ds(self.at3, self.n3)]
            self.out[pl.ds(self.at3, self.n3)] = jnp.sum(self.box3[...], axis=0)
            around(lines, line_at, lambda j: remote(part, part, self.slot + 3, line_place(j)).start())

        def share2(self):
            arrived(self.out.at[pl.ds(0, self.n2 - self.n3)], self.slot + 3)
            part = self.out.at[pl.ds(self.at2, self.n2)]
            around(planes, plane_at, lambda j: remote(part, part, self.slot + 4, plane_place(j)).start())

        def share1(self):
            arrived(self.out.at[pl.ds(0, self.n1 - self.n2)], self.slot + 4)
            part = self.out.at[pl.ds(self.at1, self.n1)]
            remote(part, part, self.slot + 5, buddy).start()

        def end(self):
            whole = self.out.at[pl.ds(0, self.n1)]
            arrived(whole, self.slot + 5)
            left(whole, self.slot + 5)
            left(self.out.at[pl.ds(0, self.n1 - self.n2)], self.slot + 4)
            left(self.out.at[pl.ds(0, self.n2 - self.n3)], self.slot + 3)
            left(self.box3.at[pl.ds(0, lines - 1)], self.slot + 2)
            left(self.box2.at[pl.ds(0, planes - 1)], self.slot + 1)
            left(self.box1, self.slot)

    first_sum = Sum(0, src0, *boxes[0:5], early)
    second_sum = Sum(1, src1, *boxes[5:10], mid)
    third_sum = Sum(2, src2, *boxes[10:15], late)

    def smooth(field, low_ref, out):
        low_high, low_low = halves(low_ref[...])
        field = field - (dot(t_low[...], low_high) + dot(t_low[...], low_low))
        out[:bt] = dot3(smo[0], field[:bt])
        out[bt:] = dot3(smo[1], field[bt:])

    @pl.when(jnp.logical_not(has_low))
    def _():
        smooth(cm[...], x_low, x_own)
    @pl.when(jnp.logical_and(jnp.logical_not(has_low), has_up))
    def _():
        remote(x_own, x_low, X_UP, UP[2]).start()

    total = local(f_own[...])
    for item in first:
        receive(*item)

    @pl.when(has_up)
    def _():
        for g in range(2):
            swap = got_swaps[g * 16:(g + 1) * 16].astype(F32)[:1]
            got_up[g * bt:(g + 1) * bt, :bt] = scaled(got_vert[g], 1.0 - swap)
            got_up[g * bt:(g + 1) * bt, bt:] = scaled(got_vert[g], swap)

    image = coupled(total, f_prev, f_next, f_low, f_up)
    x, mode_image = cm[...], image[:, :k]
    q_buf[pl.ds(me, 1), 0:1] = jnp.sum(x * mode_image, 0, keepdims=True)[None]
    q_buf[pl.ds(me, 1), 1:2] = jnp.sum(x * x, 0, keepdims=True)[None]
    others(lambda d: remote(q_buf.at[me], q_buf.at[me], QUOT, place(d)).start())

    @pl.when(has_low)
    def _():
        arrived(x_low, X_UP)
        smooth(cm[...], x_low, x_own)
    @pl.when(jnp.logical_and(has_low, has_up))
    def _():
        remote(x_own, x_low, X_UP, UP[2]).start()
    receive(p_own, p_low, P_UP, UP)
    smooth(mode_image, p_low, p_own)
    send(p_own, p_low, P_UP, UP)

    fields = jnp.concatenate([x, pv[...]], 1)
    given = jnp.concatenate([fields, image], 1)
    product = dot3(fields, given, dot_t)
    src0[0 * k:1 * k] = product[:k, :k]
    src0[1 * k:2 * k] = product[:k, k:2 * k]
    src0[2 * k:3 * k] = product[k:, k:2 * k]
    src0[3 * k:4 * k] = product[:k, 2 * k:3 * k]
    src0[4 * k:5 * k] = product[k:, 2 * k:3 * k]
    src0[5 * k:6 * k] = product[k:, 3 * k:]
    src1[0 * k:1 * k] = product[:k, 3 * k:]
    first_sum.send1()

    everyone = q_buf.at[pl.ds(0, count - 1)]
    remote(everyone, everyone, QUOT, (tier, row)).wait_recv()
    sums = jnp.sum(q_buf[...], axis=0)
    w = p_own[...] - x_own[...] * (sums[0:1] / sums[1:2])
    w_out[...] = w
    wb[...] = w.astype(BF16)
    for item in second:
        send(*item)

    product = dot3(w, jnp.concatenate([given, w], 1), dot_t)
    for at in range(5):
        src1[(at + 1) * k:(at + 2) * k] = product[:, at * k:(at + 1) * k]
    second_sum.send1()
    first_sum.send2()
    total = local(wb[...])
    second_sum.send2()
    for item in second:
        receive(*item)
    work_image = coupled(total, wb_prev, wb_next, wb_low, wb_up)
    second_sum.send3()
    first_sum.send3()
    product = dot3(jnp.concatenate([fields, w], 1), work_image, dot_t)
    src2[:3 * k] = product
    third_sum.send1()
    second_sum.share3()
    first_sum.share3()
    third_sum.send2()
    second_sum.share2()
    first_sum.share2()
    third_sum.send3()
    second_sum.share1()
    first_sum.share1()
    third_sum.share3()
    third_sum.share2()
    third_sum.share1()
    first_sum.end()
    second_sum.end()
    third_sum.end()
    remote(everyone, everyone, QUOT, (tier, row)).wait_send()
    for item in first + second:
        sent(*item)
    sent(p_own, p_low, P_UP, UP)
    sent(x_own, x_low, X_UP, UP)


def basis_kernel(
    inverse_rows, early, mid, late, stacked, ortho, projected, z_ref, a_ref, m_ref
):
    n = stacked.shape[1]
    k = n // 3

    def at(ref, i):
        return ref[i * k:(i + 1) * k]

    xw, xp, wp = at(mid, 1).T, at(early, 1), at(mid, 2)
    gram = jnp.concatenate([
        jnp.concatenate([at(early, 0), xw, xp], 1),
        jnp.concatenate([at(mid, 1), at(mid, 5), wp], 1),
        jnp.concatenate([xp.T, wp.T, at(early, 2)], 1)], 0) * inverse_rows
    inner = jnp.concatenate([
        jnp.concatenate([at(early, 3), at(late, 0), at(mid, 0)], 1),
        jnp.concatenate([at(mid, 3), at(late, 2), at(mid, 4)], 1),
        jnp.concatenate([at(early, 4), at(late, 1), at(early, 5)], 1)], 0) * inverse_rows
    below = lax.broadcasted_iota(jnp.int32, (n, n), 0)
    across = lax.broadcasted_iota(jnp.int32, (n, n), 1)
    on_diagonal = below == across
    eye = on_diagonal.astype(F32)
    weights = jnp.where(below < across, 1.0, jnp.where(on_diagonal, 0.5, 0.0))
    marked = gram * eye
    scale_row = lax.rsqrt(jnp.sum(marked, 0, keepdims=True))
    scale_column = lax.rsqrt(jnp.sum(marked, 1, keepdims=True))
    a_ref[...] = gram * scale_row * scale_column

    def error(z, split):
        a = a_ref[...]
        if split:
            return dot3(z, dot3(a, z), dot_t) - eye
        z = z.astype(BF16)
        return dot_t(z, dot(a.astype(BF16), z).astype(BF16)) - eye

    z_ref[...] = eye - (a_ref[...] - eye) * weights
    for _ in range(2):
        z = z_ref[...]
        move = error(z, False) * weights
        z_ref[...] = z - dot(z.astype(BF16), move.astype(BF16))

    def going(state):
        return jnp.logical_and(state[0] < 8, jnp.logical_not(state[1] < 2e-4))

    def step(state):
        z = z_ref[...]
        now = error(z, True)
        z_ref[...] = z - dot3(z, now * weights)
        return state[0] + 1, jnp.max(jnp.abs(now))

    _, left = lax.while_loop(going, step, (jnp.int32(0), jnp.float32(1.0)))
    lowest = jnp.min(jnp.where(on_diagonal, z_ref[...], 1.0))
    good = jnp.logical_and(left < 2e-4, lowest > 0.0)

    @pl.when(jnp.logical_not(good))
    def _():
        m_ref[...] = eye
        rows_at = lax.broadcasted_iota(jnp.int32, (n, 1), 0)

        def column(j, carry):
            row_a, row_m = a_ref[pl.ds(j, 1), :], m_ref[pl.ds(j, 1), :]
            a = a_ref[...]
            cut = jnp.sum(jnp.where(across == j, a, 0.0), 1, keepdims=True)
            pivot = jnp.sum(jnp.where(rows_at == j, cut, 0.0), 0, keepdims=True)
            factor = lax.rsqrt(pivot)
            row_a, row_m, cut = row_a * factor, row_m * factor, jnp.where(rows_at > j, cut * factor, 0.0)
            a_ref[...] = a - cut * row_a
            m_ref[...] = m_ref[...] - cut * row_m
            m_ref[pl.ds(j, 1), :] = row_m
            return carry

        lax.fori_loop(0, n, column, 0)
        z_ref[...] = m_ref[...].T

    inverse = z_ref[...] * scale_column
    high, low = halves(inverse)
    s_high, s_low = halves(stacked[...])
    ortho[...] = dot(s_high, high) + (dot(s_high, low) + dot(s_low, high))
    half = dot3(inner, inverse)
    projected[...] = dot3(inverse, half, dot_t)


def vmem(count):
    return [pl.BlockSpec(memory_space=pltpu.VMEM)] * count


def on_device(
    current_modes, previous, diag_tiles, lateral_tiles, lateral_index, vertical_tiles, vertical_index, smoother
):
    tiers, rows = lax.axis_size("tier"), lax.axis_size("row")
    count = tiers * rows
    height, k = current_modes.shape
    bt = diag_tiles.shape[-1]
    unit = 8 * count
    totals = [-(-blocks * k // unit) * unit for blocks in (6, 6, 3)]
    boxes = []
    for total in totals:
        n1 = total // 2
        n2 = n1 // (2 * tiers)
        n3 = n2 // (rows // 4)
        for shape in ((n1, k), (n2, k), (n1, k), (2 * tiers, n2, k), (rows // 4, n3, k)):
            boxes.append(pltpu.VMEM(shape, F32))
    smem = pl.BlockSpec(memory_space=pltpu.SMEM)
    hbm = pl.BlockSpec(memory_space=pltpu.HBM)
    pair = pltpu.VMEM((height, 2 * k), BF16)
    single = pltpu.VMEM((height, k), BF16)
    tall = pltpu.VMEM((height, bt), BF16)
    square = pltpu.VMEM((height, height), BF16)
    wide = pltpu.VMEM((height, k), F32)
    stacked, early, mid, late = pl.pallas_call(
        functools.partial(step_kernel, tiers, rows),
        out_shape=[
            jax.ShapeDtypeStruct((height, 3 * k), F32)] + [
            jax.ShapeDtypeStruct((total, k), F32) for total in totals],
        in_specs=[hbm, hbm, hbm, hbm, smem, hbm, smem, hbm],
        out_specs=vmem(4),
        scratch_shapes=[
            pltpu.VMEM((2, bt, bt), BF16), pltpu.VMEM((2, 2, bt, bt), BF16), pltpu.VMEM((2, bt, bt), BF16),
            pltpu.VMEM((2, bt, bt), F32), pltpu.SemaphoreType.DMA((6,)),
            pltpu.VMEM((32, bt), BF16), pltpu.VMEM((32, bt), BF16), pltpu.VMEM((2, bt, bt), BF16),
            pair, pair, pair, pair, pair,
            tall, tall, square, tall, tall, square,
            wide, wide, wide, wide, single, single, single, single, single,
            pltpu.VMEM((count, 8, k), F32),
        ] + [pltpu.VMEM((total, k), F32) for total in totals] + [
            pltpu.SemaphoreType.DMA((SEMS,)), pltpu.SemaphoreType.DMA((SEMS,))] + boxes,
        compiler_params=pltpu.CompilerParams(
            collective_id=0, has_side_effects=True, vmem_limit_bytes=60 * 2**20),
        name="step",
    )(
        current_modes, previous, diag_tiles[0, 0], lateral_tiles[0, 0], lateral_index[0, 0],
        vertical_tiles[0, 0], vertical_index[0, 0], smoother[0, 0])
    n = 3 * k
    full = pltpu.VMEM((n, n), F32)
    return pl.pallas_call(
        functools.partial(basis_kernel, 1.0 / (height * count)),
        out_shape=[jax.ShapeDtypeStruct((height, n), F32), jax.ShapeDtypeStruct((n, n), F32)],
        in_specs=vmem(4),
        out_specs=vmem(2),
        scratch_shapes=[full, full, full],
        compiler_params=pltpu.CompilerParams(vmem_limit_bytes=60 * 2**20),
        name="basis",
    )(early, mid, late, stacked)


def solution(mesh):
    placed = (
        P(("tier", "row"), None),
        P(("tier", "row"), None),
        P("tier", "row", None, None, None),
        P("tier", "row", None, None, None, None),
        P("tier", "row", None, None),
        P("tier", "row", None, None, None),
        P("tier", "row", None),
        P("tier", "row", None, None, None),
    )
    return jax.shard_map(
        on_device,
        mesh=mesh,
        in_specs=placed,
        out_specs=(P(("tier", "row"), None), P()),
        check_vma=False,
    )
```

```python
import functools

import jax
import jax.numpy as jnp
from jax import lax
from jax.experimental import pallas as pl
from jax.experimental.pallas import tpu as pltpu
from jax.sharding import PartitionSpec as P

F32 = jnp.float32
BF16 = jnp.bfloat16
MESH = pl.DeviceIdType.MESH


def dot(a, b):
    return jnp.dot(a, b, preferred_element_type=F32)


def dot_t(a, b):
    return lax.dot_general(a, b, (((0,), (0,)), ((), ())), preferred_element_type=F32)


def halves(x):
    high = x.astype(BF16)
    return high, (x - high.astype(F32)).astype(BF16)


def dot3(a, b, product=dot):
    (a_high, a_low), (b_high, b_low) = halves(a), halves(b)
    return product(a_high, b_high) + (product(a_high, b_low) + product(a_low, b_high))


def flag(condition):
    return jnp.where(condition, 1.0, 0.0).astype(F32)


def scaled(tile, factor):
    return (tile.astype(F32) * factor).astype(BF16)


F_PREV, F_NEXT, F_LOW, F_UP, T_PREV, T_NEXT, T_LOW, P_UP, W_PREV, W_NEXT, W_LOW, W_UP, QUOT, X_UP, FLAG_LOW = range(15)
SUM_AT = 15
SEMS = SUM_AT + 18


def step_kernel(
    tiers, rows,
    cm_in, pv_in, diag_in, lat_in, lat_at, vert_in, vert_at, smo_in,
    stacked, early, mid, late,
    diag, lat, vert, smo, load_sem, swaps, got_swaps, got_vert,
    f_own, f_prev, f_next, f_low, f_up,
    t_prev, t_next, t_low, got_prev, got_next, got_up,
    p_own, p_low, x_own, x_low, wb, wb_prev, wb_next, wb_low, wb_up,
    q_buf, src0, src1, src2, send_sem, recv_sem, *boxes,
):
    tier, row = lax.axis_index("tier"), lax.axis_index("row")
    count = tiers * rows
    me = tier * rows + row
    bt = diag.shape[-1]
    k = cm_in.shape[1]
    cm, w_out, pv = [stacked.at[:, i * k:(i + 1) * k] for i in range(3)]
    loads = [
        pltpu.make_async_copy(source, target, load_sem.at[i]) for i, (source, target) in enumerate(
            [(cm_in, cm), (pv_in, pv), (lat_in, lat), (vert_in, vert), (diag_in, diag), (smo_in, smo)])]
    for load in loads:
        load.start()

    def place(d):
        return (lax.div(d, rows), lax.rem(d, rows))

    def others(body):
        def step(i, carry):
            body(lax.rem(me + i, count))
            return carry
        lax.fori_loop(1, count, step, 0)

    barrier = pltpu.get_barrier_semaphore()
    others(lambda d: pl.semaphore_signal(barrier, inc=1, device_id=place(d), device_id_type=MESH))

    def remote(src, dst, slot, device):
        return pltpu.make_async_remote_copy(
            src_ref=src, dst_ref=dst, send_sem=send_sem.at[slot], recv_sem=recv_sem.at[slot],
            device_id=device, device_id_type=MESH)

    has_prev, has_next = row > 0, row < rows - 1
    has_low, has_up = tier > 0, tier < tiers - 1
    PREV, NEXT = (has_prev, has_next, (tier, row - 1)), (has_next, has_prev, (tier, row + 1))
    LOW, UP = (has_low, has_up, (tier - 1, row)), (has_up, has_low, (tier + 1, row))

    def send(src, dst, slot, way):
        @pl.when(way[0])
        def _():
            remote(src, dst, slot, way[2]).start()

    def receive(src, dst, slot, way):
        @pl.when(way[1])
        def _():
            remote(src, dst, slot, (tier, row)).wait_recv()

    def sent(src, dst, slot, way):
        @pl.when(way[0])
        def _():
            remote(src, dst, slot, (tier, row)).wait_send()

    for load in loads:
        load.wait()
    f_own[:, :k] = cm[...].astype(BF16)
    f_own[:, k:] = pv[...].astype(BF16)
    below = flag(lat_at[1, 0] == 0)
    inner_low = 1.0 - below
    above = flag(lat_at[0, 1] == 3)
    inner_up = 1.0 - above
    t_prev[:bt] = lat[0, 0]
    t_prev[bt:] = scaled(lat[1, 0], below)
    t_next[:bt] = scaled(lat[0, 1], above)
    t_next[bt:] = lat[1, 1]
    for g in range(2):
        swap = flag(vert_at[g] == 1)
        swaps[g * 16:(g + 1) * 16] = scaled(jnp.ones((16, bt), BF16), swap)
        t_low[g * bt:(g + 1) * bt, :bt] = scaled(vert[g], 1.0 - swap)
        t_low[g * bt:(g + 1) * bt, bt:] = scaled(vert[g], swap)

    @pl.when(jnp.logical_not(has_prev))
    def _():
        f_prev[...] = jnp.zeros_like(f_prev)
        wb_prev[...] = jnp.zeros_like(wb_prev)
        got_prev[...] = jnp.zeros_like(got_prev)

    @pl.when(jnp.logical_not(has_next))
    def _():
        f_next[...] = jnp.zeros_like(f_next)
        wb_next[...] = jnp.zeros_like(wb_next)
        got_next[...] = jnp.zeros_like(got_next)

    @pl.when(jnp.logical_not(has_low))
    def _():
        f_low[...] = jnp.zeros_like(f_low)
        wb_low[...] = jnp.zeros_like(wb_low)
        p_low[...] = jnp.zeros_like(p_low)
        x_low[...] = jnp.zeros_like(x_low)

    @pl.when(jnp.logical_not(has_up))
    def _():
        f_up[...] = jnp.zeros_like(f_up)
        wb_up[...] = jnp.zeros_like(wb_up)
        got_up[...] = jnp.zeros_like(got_up)

    first = [
        (f_own, f_up, F_LOW, LOW), (f_own, f_low, F_UP, UP),
        (f_own, f_next, F_PREV, PREV), (f_own, f_prev, F_NEXT, NEXT),
        (vert, got_vert, T_LOW, LOW), (swaps, got_swaps, FLAG_LOW, LOW), (t_prev, got_next, T_PREV, PREV), (t_next, got_prev, T_NEXT, NEXT),
    ]
    second = [
        (wb, wb_up, W_LOW, LOW), (wb, wb_low, W_UP, UP),
        (wb, wb_next, W_PREV, PREV), (wb, wb_prev, W_NEXT, NEXT),
    ]
    pl.semaphore_wait(barrier, count - 1)
    for item in first:
        send(*item)

    zero = jnp.zeros((bt, bt), BF16)
    cross_up, cross_low = scaled(lat[0, 1], inner_up), scaled(lat[1, 0], inner_low)
    inner = jnp.concatenate([
        jnp.concatenate([diag[0], cross_up], 1), jnp.concatenate([cross_low, diag[1]], 1)], 0)
    crossed = jnp.concatenate([
        jnp.concatenate([zero, cross_up], 1), jnp.concatenate([cross_low, zero], 1)], 0)

    def local(own):
        return dot(inner, own) + dot_t(crossed, own)

    def coupled(total, prev, after, low, up):
        total = total + dot(t_prev[...], prev[bt:]) + dot(t_next[...], after[:bt])
        total = total + dot(t_low[...], low[...]) + dot_t(got_up[...], up[...])
        edge = jnp.concatenate([dot_t(got_prev[...], prev[...]), dot_t(got_next[...], after[...])], 0)
        return total + edge

    half_at = lax.rem(row, 2)
    plane_at = tier * 2 + lax.rem(lax.div(row, 2), 2)
    line_at = lax.div(row, 4)
    planes, lines = 2 * tiers, rows // 4
    buddy = (tier, row + 1 - 2 * half_at)

    def plane_place(j):
        return (lax.div(j, 2), line_at * 4 + lax.rem(j, 2) * 2 + half_at)

    def line_place(j):
        return (tier, j * 4 + lax.rem(row, 4))

    def around(size, own, body):
        def step(i, carry):
            body(lax.rem(own + i, size))
            return carry
        lax.fori_loop(1, size, step, 0)

    def arrived(part, slot):
        remote(part, part, slot, (tier, row)).wait_recv()

    def left(part, slot):
        remote(part, part, slot, (tier, row)).wait_send()

    class Sum:
        def __init__(self, which, src, part1, part2, box1, box2, box3, out):
            self.src, self.part1, self.part2, self.out = src, part1, part2, out
            self.box1, self.box2, self.box3 = box1, box2, box3
            self.slot = SUM_AT + 6 * which
            self.n1 = src.shape[0] // 2
            self.n2 = self.n1 // planes
            self.n3 = self.n2 // lines
            self.at1 = pl.multiple_of(half_at * self.n1, 8)
            self.at2 = pl.multiple_of(self.at1 + plane_at * self.n2, 8)
            self.at3 = pl.multiple_of(self.at2 + line_at * self.n3, 8)

        def send1(self):
            away = pl.multiple_of((1 - half_at) * self.n1, 8)
            remote(self.src.at[pl.ds(away, self.n1)], self.box1, self.slot, buddy).start()

        def send2(self):
            arrived(self.box1, self.slot)
            self.part1[...] = self.src[pl.ds(self.at1, self.n1)] + self.box1[...]
            def body(j):
                piece = self.part1.at[pl.ds(pl.multiple_of(j * self.n2, 8), self.n2)]
                remote(piece, self.box2.at[plane_at], self.slot + 1, plane_place(j)).start()
            around(planes, plane_at, body)
            mine = self.part1[pl.ds(pl.multiple_of(plane_at * self.n2, 8), self.n2)]
            self.box2[pl.ds(plane_at, 1)] = mine[None]

        def send3(self):
            arrived(self.box2.at[pl.ds(0, planes - 1)], self.slot + 1)
            self.part2[...] = jnp.sum(self.box2[...], axis=0)
            def body(j):
                piece = self.part2.at[pl.ds(pl.multiple_of(j * self.n3, 8), self.n3)]
                remote(piece, self.box3.at[line_at], self.slot + 2, line_place(j)).start()
            around(lines, line_at, body)
            mine = self.part2[pl.ds(pl.multiple_of(line_at * self.n3, 8), self.n3)]
            self.box3[pl.ds(line_at, 1)] = mine[None]

        def share3(self):
            arrived(self.box3.at[pl.ds(0, lines - 1)], self.slot + 2)
            part = self.out.at[pl.ds(self.at3, self.n3)]
            self.out[pl.ds(self.at3, self.n3)] = jnp.sum(self.box3[...], axis=0)
            around(lines, line_at, lambda j: remote(part, part, self.slot + 3, line_place(j)).start())

        def share2(self):
            arrived(self.out.at[pl.ds(0, self.n2 - self.n3)], self.slot + 3)
            part = self.out.at[pl.ds(self.at2, self.n2)]
            around(planes, plane_at, lambda j: remote(part, part, self.slot + 4, plane_place(j)).start())

        def share1(self):
            arrived(self.out.at[pl.ds(0, self.n1 - self.n2)], self.slot + 4)
            part = self.out.at[pl.ds(self.at1, self.n1)]
            remote(part, part, self.slot + 5, buddy).start()

        def end(self):
            whole = self.out.at[pl.ds(0, self.n1)]
            arrived(whole, self.slot + 5)
            left(whole, self.slot + 5)
            left(self.out.at[pl.ds(0, self.n1 - self.n2)], self.slot + 4)
            left(self.out.at[pl.ds(0, self.n2 - self.n3)], self.slot + 3)
            left(self.box3.at[pl.ds(0, lines - 1)], self.slot + 2)
            left(self.box2.at[pl.ds(0, planes - 1)], self.slot + 1)
            left(self.box1, self.slot)

    first_sum = Sum(0, src0, *boxes[0:5], early)
    second_sum = Sum(1, src1, *boxes[5:10], mid)
    third_sum = Sum(2, src2, *boxes[10:15], late)

    def smooth(field, low_ref, out):
        low_high, low_low = halves(low_ref[...])
        field = field - (dot(t_low[...], low_high) + dot(t_low[...], low_low))
        out[:bt] = dot3(smo[0], field[:bt])
        out[bt:] = dot3(smo[1], field[bt:])

    @pl.when(jnp.logical_not(has_low))
    def _():
        smooth(cm[...], x_low, x_own)
    @pl.when(jnp.logical_and(jnp.logical_not(has_low), has_up))
    def _():
        remote(x_own, x_low, X_UP, UP[2]).start()

    total = local(f_own[...])
    for item in first:
        receive(*item)

    @pl.when(has_up)
    def _():
        for g in range(2):
            swap = got_swaps[g * 16:(g + 1) * 16].astype(F32)[:1]
            got_up[g * bt:(g + 1) * bt, :bt] = scaled(got_vert[g], 1.0 - swap)
            got_up[g * bt:(g + 1) * bt, bt:] = scaled(got_vert[g], swap)

    image = coupled(total, f_prev, f_next, f_low, f_up)
    x, mode_image = cm[...], image[:, :k]
    q_buf[pl.ds(me, 1), 0:1] = jnp.sum(x * mode_image, 0, keepdims=True)[None]
    q_buf[pl.ds(me, 1), 1:2] = jnp.sum(x * x, 0, keepdims=True)[None]
    others(lambda d: remote(q_buf.at[me], q_buf.at[me], QUOT, place(d)).start())

    @pl.when(has_low)
    def _():
        arrived(x_low, X_UP)
        smooth(cm[...], x_low, x_own)
    @pl.when(jnp.logical_and(has_low, has_up))
    def _():
        remote(x_own, x_low, X_UP, UP[2]).start()
    receive(p_own, p_low, P_UP, UP)
    smooth(mode_image, p_low, p_own)
    send(p_own, p_low, P_UP, UP)

    fields = jnp.concatenate([x, pv[...]], 1)
    given = jnp.concatenate([fields, image], 1)
    product = dot3(fields, given, dot_t)
    src0[0 * k:1 * k] = product[:k, :k]
    src0[1 * k:2 * k] = product[:k, k:2 * k]
    src0[2 * k:3 * k] = product[k:, k:2 * k]
    src0[3 * k:4 * k] = product[:k, 2 * k:3 * k]
    src0[4 * k:5 * k] = product[k:, 2 * k:3 * k]
    src0[5 * k:6 * k] = product[k:, 3 * k:]
    src1[0 * k:1 * k] = product[:k, 3 * k:]
    first_sum.send1()

    everyone = q_buf.at[pl.ds(0, count - 1)]
    remote(everyone, everyone, QUOT, (tier, row)).wait_recv()
    sums = jnp.sum(q_buf[...], axis=0)
    w = p_own[...] - x_own[...] * (sums[0:1] / sums[1:2])
    w_out[...] = w
    wb[...] = w.astype(BF16)
    for item in second:
        send(*item)

    product = dot3(w, jnp.concatenate([given, w], 1), dot_t)
    for at in range(5):
        src1[(at + 1) * k:(at + 2) * k] = product[:, at * k:(at + 1) * k]
    second_sum.send1()
    first_sum.send2()
    total = local(wb[...])
    for item in second:
        receive(*item)
    work_image = coupled(total, wb_prev, wb_next, wb_low, wb_up)
    product = dot3(jnp.concatenate([fields, w], 1), work_image, dot_t)
    src2[:3 * k] = product
    third_sum.send1()
    second_sum.send2()
    first_sum.send3()
    third_sum.send2()
    second_sum.send3()
    first_sum.share3()
    third_sum.send3()
    second_sum.share3()
    first_sum.share2()
    third_sum.share3()
    second_sum.share2()
    first_sum.share1()
    third_sum.share2()
    second_sum.share1()
    third_sum.share1()
    first_sum.end()
    second_sum.end()
    third_sum.end()
    remote(everyone, everyone, QUOT, (tier, row)).wait_send()
    for item in first + second:
        sent(*item)
    sent(p_own, p_low, P_UP, UP)
    sent(x_own, x_low, X_UP, UP)


def basis_kernel(
    inverse_rows, early, mid, late, stacked, ortho, projected, z_ref, a_ref, m_ref
):
    n = stacked.shape[1]
    k = n // 3

    def at(ref, i):
        return ref[i * k:(i + 1) * k]

    xw, xp, wp = at(mid, 1).T, at(early, 1), at(mid, 2)
    gram = jnp.concatenate([
        jnp.concatenate([at(early, 0), xw, xp], 1),
        jnp.concatenate([at(mid, 1), at(mid, 5), wp], 1),
        jnp.concatenate([xp.T, wp.T, at(early, 2)], 1)], 0) * inverse_rows
    inner = jnp.concatenate([
        jnp.concatenate([at(early, 3), at(late, 0), at(mid, 0)], 1),
        jnp.concatenate([at(mid, 3), at(late, 2), at(mid, 4)], 1),
        jnp.concatenate([at(early, 4), at(late, 1), at(early, 5)], 1)], 0) * inverse_rows
    below = lax.broadcasted_iota(jnp.int32, (n, n), 0)
    across = lax.broadcasted_iota(jnp.int32, (n, n), 1)
    on_diagonal = below == across
    eye = on_diagonal.astype(F32)
    weights = jnp.where(below < across, 1.0, jnp.where(on_diagonal, 0.5, 0.0))
    marked = gram * eye
    scale_row = lax.rsqrt(jnp.sum(marked, 0, keepdims=True))
    scale_column = lax.rsqrt(jnp.sum(marked, 1, keepdims=True))
    a_ref[...] = gram * scale_row * scale_column

    def error(z, split):
        a = a_ref[...]
        if split:
            return dot3(z, dot3(a, z), dot_t) - eye
        z = z.astype(BF16)
        return dot_t(z, dot(a.astype(BF16), z).astype(BF16)) - eye

    z_ref[...] = eye - (a_ref[...] - eye) * weights
    for _ in range(2):
        z = z_ref[...]
        move = error(z, False) * weights
        z_ref[...] = z - dot(z.astype(BF16), move.astype(BF16))

    def going(state):
        return jnp.logical_and(state[0] < 8, jnp.logical_not(state[1] < 2e-4))

    def step(state):
        z = z_ref[...]
        now = error(z, True)
        z_ref[...] = z - dot3(z, now * weights)
        return state[0] + 1, jnp.max(jnp.abs(now))

    _, left = lax.while_loop(going, step, (jnp.int32(0), jnp.float32(1.0)))
    lowest = jnp.min(jnp.where(on_diagonal, z_ref[...], 1.0))
    good = jnp.logical_and(left < 2e-4, lowest > 0.0)

    @pl.when(jnp.logical_not(good))
    def _():
        m_ref[...] = eye
        rows_at = lax.broadcasted_iota(jnp.int32, (n, 1), 0)

        def column(j, carry):
            row_a, row_m = a_ref[pl.ds(j, 1), :], m_ref[pl.ds(j, 1), :]
            a = a_ref[...]
            cut = jnp.sum(jnp.where(across == j, a, 0.0), 1, keepdims=True)
            pivot = jnp.sum(jnp.where(rows_at == j, cut, 0.0), 0, keepdims=True)
            factor = lax.rsqrt(pivot)
            row_a, row_m, cut = row_a * factor, row_m * factor, jnp.where(rows_at > j, cut * factor, 0.0)
            a_ref[...] = a - cut * row_a
            m_ref[...] = m_ref[...] - cut * row_m
            m_ref[pl.ds(j, 1), :] = row_m
            return carry

        lax.fori_loop(0, n, column, 0)
        z_ref[...] = m_ref[...].T

    inverse = z_ref[...] * scale_column
    high, low = halves(inverse)
    s_high, s_low = halves(stacked[...])
    ortho[...] = dot(s_high, high) + (dot(s_high, low) + dot(s_low, high))
    half = dot3(inner, inverse)
    projected[...] = dot3(inverse, half, dot_t)


def vmem(count):
    return [pl.BlockSpec(memory_space=pltpu.VMEM)] * count


def on_device(
    current_modes, previous, diag_tiles, lateral_tiles, lateral_index, vertical_tiles, vertical_index, smoother
):
    tiers, rows = lax.axis_size("tier"), lax.axis_size("row")
    count = tiers * rows
    height, k = current_modes.shape
    bt = diag_tiles.shape[-1]
    unit = 8 * count
    totals = [-(-blocks * k // unit) * unit for blocks in (6, 6, 3)]
    boxes = []
    for total in totals:
        n1 = total // 2
        n2 = n1 // (2 * tiers)
        n3 = n2 // (rows // 4)
        for shape in ((n1, k), (n2, k), (n1, k), (2 * tiers, n2, k), (rows // 4, n3, k)):
            boxes.append(pltpu.VMEM(shape, F32))
    smem = pl.BlockSpec(memory_space=pltpu.SMEM)
    hbm = pl.BlockSpec(memory_space=pltpu.HBM)
    pair = pltpu.VMEM((height, 2 * k), BF16)
    single = pltpu.VMEM((height, k), BF16)
    tall = pltpu.VMEM((height, bt), BF16)
    square = pltpu.VMEM((height, height), BF16)
    wide = pltpu.VMEM((height, k), F32)
    stacked, early, mid, late = pl.pallas_call(
        functools.partial(step_kernel, tiers, rows),
        out_shape=[
            jax.ShapeDtypeStruct((height, 3 * k), F32)] + [
            jax.ShapeDtypeStruct((total, k), F32) for total in totals],
        in_specs=[hbm, hbm, hbm, hbm, smem, hbm, smem, hbm],
        out_specs=vmem(4),
        scratch_shapes=[
            pltpu.VMEM((2, bt, bt), BF16), pltpu.VMEM((2, 2, bt, bt), BF16), pltpu.VMEM((2, bt, bt), BF16),
            pltpu.VMEM((2, bt, bt), F32), pltpu.SemaphoreType.DMA((6,)),
            pltpu.VMEM((32, bt), BF16), pltpu.VMEM((32, bt), BF16), pltpu.VMEM((2, bt, bt), BF16),
            pair, pair, pair, pair, pair,
            tall, tall, square, tall, tall, square,
            wide, wide, wide, wide, single, single, single, single, single,
            pltpu.VMEM((count, 8, k), F32),
        ] + [pltpu.VMEM((total, k), F32) for total in totals] + [
            pltpu.SemaphoreType.DMA((SEMS,)), pltpu.SemaphoreType.DMA((SEMS,))] + boxes,
        compiler_params=pltpu.CompilerParams(
            collective_id=0, has_side_effects=True, vmem_limit_bytes=60 * 2**20),
        name="step",
    )(
        current_modes, previous, diag_tiles[0, 0], lateral_tiles[0, 0], lateral_index[0, 0],
        vertical_tiles[0, 0], vertical_index[0, 0], smoother[0, 0])
    n = 3 * k
    full = pltpu.VMEM((n, n), F32)
    return pl.pallas_call(
        functools.partial(basis_kernel, 1.0 / (height * count)),
        out_shape=[jax.ShapeDtypeStruct((height, n), F32), jax.ShapeDtypeStruct((n, n), F32)],
        in_specs=vmem(4),
        out_specs=vmem(2),
        scratch_shapes=[full, full, full],
        compiler_params=pltpu.CompilerParams(vmem_limit_bytes=60 * 2**20),
        name="basis",
    )(early, mid, late, stacked)


def solution(mesh):
    placed = (
        P(("tier", "row"), None),
        P(("tier", "row"), None),
        P("tier", "row", None, None, None),
        P("tier", "row", None, None, None, None),
        P("tier", "row", None, None),
        P("tier", "row", None, None, None),
        P("tier", "row", None),
        P("tier", "row", None, None, None),
    )
    return jax.shard_map(
        on_device,
        mesh=mesh,
        in_specs=placed,
        out_specs=(P(("tier", "row"), None), P()),
        check_vma=False,
    )
```

```python
import functools

import jax
import jax.numpy as jnp
from jax import lax
from jax.experimental import pallas as pl
from jax.experimental.pallas import tpu as pltpu
from jax.sharding import PartitionSpec as P

F32 = jnp.float32
BF16 = jnp.bfloat16
MESH = pl.DeviceIdType.MESH


def dot(a, b):
    return jnp.dot(a, b, preferred_element_type=F32)


def dot_t(a, b):
    return lax.dot_general(a, b, (((0,), (0,)), ((), ())), preferred_element_type=F32)


def halves(x):
    high = x.astype(BF16)
    return high, (x - high.astype(F32)).astype(BF16)


def dot3(a, b, product=dot):
    (a_high, a_low), (b_high, b_low) = halves(a), halves(b)
    return product(a_high, b_high) + (product(a_high, b_low) + product(a_low, b_high))


def flag(condition):
    return jnp.where(condition, 1.0, 0.0).astype(F32)


def scaled(tile, factor):
    return (tile.astype(F32) * factor).astype(BF16)


F_PREV, F_NEXT, F_LOW, F_UP, T_PREV, T_NEXT, T_LOW, P_UP, W_PREV, W_NEXT, W_LOW, W_UP, QUOT, X_UP, FLAG_LOW = range(15)
SUM_AT = 15
SEMS = SUM_AT + 18


def step_kernel(
    tiers, rows,
    cm_in, pv_in, diag_in, lat_in, lat_at, vert_in, vert_at, smo_in,
    stacked, early, mid, late,
    diag, lat, vert, smo, load_sem, swaps, got_swaps, got_vert,
    f_own, f_prev, f_next, f_low, f_up,
    t_prev, t_next, t_low, got_prev, got_next, got_up,
    p_own, p_low, x_own, x_low, wb, wb_prev, wb_next, wb_low, wb_up,
    q_buf, src0, src1, src2, send_sem, recv_sem, *boxes,
):
    tier, row = lax.axis_index("tier"), lax.axis_index("row")
    count = tiers * rows
    me = tier * rows + row
    bt = diag.shape[-1]
    k = cm_in.shape[1]
    cm, w_out, pv = [stacked.at[:, i * k:(i + 1) * k] for i in range(3)]
    loads = [
        pltpu.make_async_copy(source, target, load_sem.at[i]) for i, (source, target) in enumerate(
            [(cm_in, cm), (pv_in, pv), (lat_in, lat), (vert_in, vert), (diag_in, diag), (smo_in, smo)])]
    for load in loads:
        load.start()

    def place(d):
        return (lax.div(d, rows), lax.rem(d, rows))

    def others(body):
        def step(i, carry):
            body(lax.rem(me + i, count))
            return carry
        lax.fori_loop(1, count, step, 0)

    barrier = pltpu.get_barrier_semaphore()
    others(lambda d: pl.semaphore_signal(barrier, inc=1, device_id=place(d), device_id_type=MESH))

    def remote(src, dst, slot, device):
        return pltpu.make_async_remote_copy(
            src_ref=src, dst_ref=dst, send_sem=send_sem.at[slot], recv_sem=recv_sem.at[slot],
            device_id=device, device_id_type=MESH)

    has_prev, has_next = row > 0, row < rows - 1
    has_low, has_up = tier > 0, tier < tiers - 1
    PREV, NEXT = (has_prev, has_next, (tier, row - 1)), (has_next, has_prev, (tier, row + 1))
    LOW, UP = (has_low, has_up, (tier - 1, row)), (has_up, has_low, (tier + 1, row))

    def send(src, dst, slot, way):
        @pl.when(way[0])
        def _():
            remote(src, dst, slot, way[2]).start()

    def receive(src, dst, slot, way):
        @pl.when(way[1])
        def _():
            remote(src, dst, slot, (tier, row)).wait_recv()

    def sent(src, dst, slot, way):
        @pl.when(way[0])
        def _():
            remote(src, dst, slot, (tier, row)).wait_send()

    for load in loads:
        load.wait()
    f_own[:, :k] = cm[...].astype(BF16)
    f_own[:, k:] = pv[...].astype(BF16)
    below = flag(lat_at[1, 0] == 0)
    inner_low = 1.0 - below
    above = flag(lat_at[0, 1] == 3)
    inner_up = 1.0 - above
    t_prev[:bt] = lat[0, 0]
    t_prev[bt:] = scaled(lat[1, 0], below)
    t_next[:bt] = scaled(lat[0, 1], above)
    t_next[bt:] = lat[1, 1]
    for g in range(2):
        swap = flag(vert_at[g] == 1)
        swaps[g * 16:(g + 1) * 16] = scaled(jnp.ones((16, bt), BF16), swap)
        t_low[g * bt:(g + 1) * bt, :bt] = scaled(vert[g], 1.0 - swap)
        t_low[g * bt:(g + 1) * bt, bt:] = scaled(vert[g], swap)

    @pl.when(jnp.logical_not(has_prev))
    def _():
        f_prev[...] = jnp.zeros_like(f_prev)
        wb_prev[...] = jnp.zeros_like(wb_prev)
        got_prev[...] = jnp.zeros_like(got_prev)

    @pl.when(jnp.logical_not(has_next))
    def _():
        f_next[...] = jnp.zeros_like(f_next)
        wb_next[...] = jnp.zeros_like(wb_next)
        got_next[...] = jnp.zeros_like(got_next)

    @pl.when(jnp.logical_not(has_low))
    def _():
        f_low[...] = jnp.zeros_like(f_low)
        wb_low[...] = jnp.zeros_like(wb_low)
        p_low[...] = jnp.zeros_like(p_low)
        x_low[...] = jnp.zeros_like(x_low)

    @pl.when(jnp.logical_not(has_up))
    def _():
        f_up[...] = jnp.zeros_like(f_up)
        wb_up[...] = jnp.zeros_like(wb_up)
        got_up[...] = jnp.zeros_like(got_up)

    first = [
        (f_own, f_up, F_LOW, LOW), (f_own, f_low, F_UP, UP),
        (f_own, f_next, F_PREV, PREV), (f_own, f_prev, F_NEXT, NEXT),
        (vert, got_vert, T_LOW, LOW), (swaps, got_swaps, FLAG_LOW, LOW), (t_prev, got_next, T_PREV, PREV), (t_next, got_prev, T_NEXT, NEXT),
    ]
    second = [
        (wb, wb_up, W_LOW, LOW), (wb, wb_low, W_UP, UP),
        (wb, wb_next, W_PREV, PREV), (wb, wb_prev, W_NEXT, NEXT),
    ]
    pl.semaphore_wait(barrier, count - 1)
    for item in first:
        send(*item)

    zero = jnp.zeros((bt, bt), BF16)
    cross_up, cross_low = scaled(lat[0, 1], inner_up), scaled(lat[1, 0], inner_low)
    inner = jnp.concatenate([
        jnp.concatenate([diag[0], cross_up], 1), jnp.concatenate([cross_low, diag[1]], 1)], 0)
    crossed = jnp.concatenate([
        jnp.concatenate([zero, cross_up], 1), jnp.concatenate([cross_low, zero], 1)], 0)

    def local(own):
        return dot(inner, own) + dot_t(crossed, own)

    def coupled(total, prev, after, low, up):
        total = total + dot(t_prev[...], prev[bt:]) + dot(t_next[...], after[:bt])
        total = total + dot(t_low[...], low[...]) + dot_t(got_up[...], up[...])
        edge = jnp.concatenate([dot_t(got_prev[...], prev[...]), dot_t(got_next[...], after[...])], 0)
        return total + edge

    half_at = lax.rem(row, 2)
    plane_at = tier * 2 + lax.rem(lax.div(row, 2), 2)
    line_at = lax.div(row, 4)
    planes, lines = 2 * tiers, rows // 4
    buddy = (tier, row + 1 - 2 * half_at)

    def plane_place(j):
        return (lax.div(j, 2), line_at * 4 + lax.rem(j, 2) * 2 + half_at)

    def line_place(j):
        return (tier, j * 4 + lax.rem(row, 4))

    def around(size, own, body):
        def step(i, carry):
            body(lax.rem(own + i, size))
            return carry
        lax.fori_loop(1, size, step, 0)

    def arrived(part, slot):
        remote(part, part, slot, (tier, row)).wait_recv()

    def left(part, slot):
        remote(part, part, slot, (tier, row)).wait_send()

    class Sum:
        def __init__(self, which, src, part1, part2, box1, box2, box3, out):
            self.src, self.part1, self.part2, self.out = src, part1, part2, out
            self.box1, self.box2, self.box3 = box1, box2, box3
            self.slot = SUM_AT + 6 * which
            self.n1 = src.shape[0] // 2
            self.n2 = self.n1 // planes
            self.n3 = self.n2 // lines
            self.at1 = pl.multiple_of(half_at * self.n1, 8)
            self.at2 = pl.multiple_of(self.at1 + plane_at * self.n2, 8)
            self.at3 = pl.multiple_of(self.at2 + line_at * self.n3, 8)

        def send1(self):
            away = pl.multiple_of((1 - half_at) * self.n1, 8)
            remote(self.src.at[pl.ds(away, self.n1)], self.box1, self.slot, buddy).start()

        def send2(self):
            arrived(self.box1, self.slot)
            self.part1[...] = self.src[pl.ds(self.at1, self.n1)] + self.box1[...]
            def body(j):
                piece = self.part1.at[pl.ds(pl.multiple_of(j * self.n2, 8), self.n2)]
                remote(piece, self.box2.at[plane_at], self.slot + 1, plane_place(j)).start()
            around(planes, plane_at, body)
            mine = self.part1[pl.ds(pl.multiple_of(plane_at * self.n2, 8), self.n2)]
            self.box2[pl.ds(plane_at, 1)] = mine[None]

        def send3(self):
            arrived(self.box2.at[pl.ds(0, planes - 1)], self.slot + 1)
            self.part2[...] = jnp.sum(self.box2[...], axis=0)
            def body(j):
                piece = self.part2.at[pl.ds(pl.multiple_of(j * self.n3, 8), self.n3)]
                remote(piece, self.box3.at[line_at], self.slot + 2, line_place(j)).start()
            around(lines, line_at, body)
            mine = self.part2[pl.ds(pl.multiple_of(line_at * self.n3, 8), self.n3)]
            self.box3[pl.ds(line_at, 1)] = mine[None]

        def share3(self):
            arrived(self.box3.at[pl.ds(0, lines - 1)], self.slot + 2)
            part = self.out.at[pl.ds(self.at3, self.n3)]
            self.out[pl.ds(self.at3, self.n3)] = jnp.sum(self.box3[...], axis=0)
            around(lines, line_at, lambda j: remote(part, part, self.slot + 3, line_place(j)).start())

        def share2(self):
            arrived(self.out.at[pl.ds(0, self.n2 - self.n3)], self.slot + 3)
            part = self.out.at[pl.ds(self.at2, self.n2)]
            around(planes, plane_at, lambda j: remote(part, part, self.slot + 4, plane_place(j)).start())

        def share1(self):
            arrived(self.out.at[pl.ds(0, self.n1 - self.n2)], self.slot + 4)
            part = self.out.at[pl.ds(self.at1, self.n1)]
            remote(part, part, self.slot + 5, buddy).start()

        def end(self):
            whole = self.out.at[pl.ds(0, self.n1)]
            arrived(whole, self.slot + 5)
            left(whole, self.slot + 5)
            left(self.out.at[pl.ds(0, self.n1 - self.n2)], self.slot + 4)
            left(self.out.at[pl.ds(0, self.n2 - self.n3)], self.slot + 3)
            left(self.box3.at[pl.ds(0, lines - 1)], self.slot + 2)
            left(self.box2.at[pl.ds(0, planes - 1)], self.slot + 1)
            left(self.box1, self.slot)

    first_sum = Sum(0, src0, *boxes[0:5], early)
    second_sum = Sum(1, src1, *boxes[5:10], mid)
    third_sum = Sum(2, src2, *boxes[10:15], late)

    def smooth(field, low_ref, out):
        low_high, low_low = halves(low_ref[...])
        field = field - (dot(t_low[...], low_high) + dot(t_low[...], low_low))
        out[:bt] = dot3(smo[0], field[:bt])
        out[bt:] = dot3(smo[1], field[bt:])

    @pl.when(jnp.logical_not(has_low))
    def _():
        smooth(cm[...], x_low, x_own)
    @pl.when(jnp.logical_and(jnp.logical_not(has_low), has_up))
    def _():
        remote(x_own, x_low, X_UP, UP[2]).start()

    total = local(f_own[...])
    for item in first:
        receive(*item)

    @pl.when(has_up)
    def _():
        for g in range(2):
            swap = got_swaps[g * 16:(g + 1) * 16].astype(F32)[:1]
            got_up[g * bt:(g + 1) * bt, :bt] = scaled(got_vert[g], 1.0 - swap)
            got_up[g * bt:(g + 1) * bt, bt:] = scaled(got_vert[g], swap)

    image = coupled(total, f_prev, f_next, f_low, f_up)
    x, mode_image = cm[...], image[:, :k]
    q_buf[pl.ds(me, 1), 0:1] = jnp.sum(x * mode_image, 0, keepdims=True)[None]
    q_buf[pl.ds(me, 1), 1:2] = jnp.sum(x * x, 0, keepdims=True)[None]
    others(lambda d: remote(q_buf.at[me], q_buf.at[me], QUOT, place(d)).start())

    @pl.when(has_low)
    def _():
        arrived(x_low, X_UP)
        smooth(cm[...], x_low, x_own)
    @pl.when(jnp.logical_and(has_low, has_up))
    def _():
        remote(x_own, x_low, X_UP, UP[2]).start()
    receive(p_own, p_low, P_UP, UP)
    smooth(mode_image, p_low, p_own)
    send(p_own, p_low, P_UP, UP)

    everyone = q_buf.at[pl.ds(0, count - 1)]
    remote(everyone, everyone, QUOT, (tier, row)).wait_recv()
    sums = jnp.sum(q_buf[...], axis=0)
    w = p_own[...] - x_own[...] * (sums[0:1] / sums[1:2])
    w_out[...] = w
    wb[...] = w.astype(BF16)
    for item in second:
        send(*item)

    fields = jnp.concatenate([x, pv[...]], 1)
    given = jnp.concatenate([fields, image], 1)
    product = dot3(fields, given, dot_t)
    src0[0 * k:1 * k] = product[:k, :k]
    src0[1 * k:2 * k] = product[:k, k:2 * k]
    src0[2 * k:3 * k] = product[k:, k:2 * k]
    src0[3 * k:4 * k] = product[:k, 2 * k:3 * k]
    src0[4 * k:5 * k] = product[k:, 2 * k:3 * k]
    src0[5 * k:6 * k] = product[k:, 3 * k:]
    src1[0 * k:1 * k] = product[:k, 3 * k:]
    first_sum.send1()

    product = dot3(w, jnp.concatenate([given, w], 1), dot_t)
    for at in range(5):
        src1[(at + 1) * k:(at + 2) * k] = product[:, at * k:(at + 1) * k]
    second_sum.send1()
    first_sum.send2()
    total = local(wb[...])
    for item in second:
        receive(*item)
    work_image = coupled(total, wb_prev, wb_next, wb_low, wb_up)
    product = dot3(jnp.concatenate([fields, w], 1), work_image, dot_t)
    src2[:3 * k] = product
    third_sum.send1()
    second_sum.send2()
    first_sum.send3()
    third_sum.send2()
    second_sum.send3()
    first_sum.share3()
    third_sum.send3()
    second_sum.share3()
    first_sum.share2()
    third_sum.share3()
    second_sum.share2()
    first_sum.share1()
    third_sum.share2()
    second_sum.share1()
    third_sum.share1()
    first_sum.end()
    second_sum.end()
    third_sum.end()
    remote(everyone, everyone, QUOT, (tier, row)).wait_send()
    for item in first + second:
        sent(*item)
    sent(p_own, p_low, P_UP, UP)
    sent(x_own, x_low, X_UP, UP)


def basis_kernel(
    inverse_rows, early, mid, late, stacked, ortho, projected, z_ref, a_ref, m_ref
):
    n = stacked.shape[1]
    k = n // 3

    def at(ref, i):
        return ref[i * k:(i + 1) * k]

    xw, xp, wp = at(mid, 1).T, at(early, 1), at(mid, 2)
    gram = jnp.concatenate([
        jnp.concatenate([at(early, 0), xw, xp], 1),
        jnp.concatenate([at(mid, 1), at(mid, 5), wp], 1),
        jnp.concatenate([xp.T, wp.T, at(early, 2)], 1)], 0) * inverse_rows
    inner = jnp.concatenate([
        jnp.concatenate([at(early, 3), at(late, 0), at(mid, 0)], 1),
        jnp.concatenate([at(mid, 3), at(late, 2), at(mid, 4)], 1),
        jnp.concatenate([at(early, 4), at(late, 1), at(early, 5)], 1)], 0) * inverse_rows
    below = lax.broadcasted_iota(jnp.int32, (n, n), 0)
    across = lax.broadcasted_iota(jnp.int32, (n, n), 1)
    on_diagonal = below == across
    eye = on_diagonal.astype(F32)
    weights = jnp.where(below < across, 1.0, jnp.where(on_diagonal, 0.5, 0.0))
    marked = gram * eye
    scale_row = lax.rsqrt(jnp.sum(marked, 0, keepdims=True))
    scale_column = lax.rsqrt(jnp.sum(marked, 1, keepdims=True))
    a_ref[...] = gram * scale_row * scale_column

    def error(z, split):
        a = a_ref[...]
        if split:
            return dot3(z, dot3(a, z), dot_t) - eye
        z = z.astype(BF16)
        return dot_t(z, dot(a.astype(BF16), z).astype(BF16)) - eye

    z_ref[...] = eye - (a_ref[...] - eye) * weights
    for _ in range(2):
        z = z_ref[...]
        move = error(z, False) * weights
        z_ref[...] = z - dot(z.astype(BF16), move.astype(BF16))

    def going(state):
        return jnp.logical_and(state[0] < 8, jnp.logical_not(state[1] < 2e-4))

    def step(state):
        z = z_ref[...]
        now = error(z, True)
        z_ref[...] = z - dot3(z, now * weights)
        return state[0] + 1, jnp.max(jnp.abs(now))

    _, left = lax.while_loop(going, step, (jnp.int32(0), jnp.float32(1.0)))
    lowest = jnp.min(jnp.where(on_diagonal, z_ref[...], 1.0))
    good = jnp.logical_and(left < 2e-4, lowest > 0.0)

    @pl.when(jnp.logical_not(good))
    def _():
        m_ref[...] = eye
        rows_at = lax.broadcasted_iota(jnp.int32, (n, 1), 0)

        def column(j, carry):
            row_a, row_m = a_ref[pl.ds(j, 1), :], m_ref[pl.ds(j, 1), :]
            a = a_ref[...]
            cut = jnp.sum(jnp.where(across == j, a, 0.0), 1, keepdims=True)
            pivot = jnp.sum(jnp.where(rows_at == j, cut, 0.0), 0, keepdims=True)
            factor = lax.rsqrt(pivot)
            row_a, row_m, cut = row_a * factor, row_m * factor, jnp.where(rows_at > j, cut * factor, 0.0)
            a_ref[...] = a - cut * row_a
            m_ref[...] = m_ref[...] - cut * row_m
            m_ref[pl.ds(j, 1), :] = row_m
            return carry

        lax.fori_loop(0, n, column, 0)
        z_ref[...] = m_ref[...].T

    inverse = z_ref[...] * scale_column
    high, low = halves(inverse)
    s_high, s_low = halves(stacked[...])
    ortho[...] = dot(s_high, high) + (dot(s_high, low) + dot(s_low, high))
    half = dot3(inner, inverse)
    projected[...] = dot3(inverse, half, dot_t)


def vmem(count):
    return [pl.BlockSpec(memory_space=pltpu.VMEM)] * count


def on_device(
    current_modes, previous, diag_tiles, lateral_tiles, lateral_index, vertical_tiles, vertical_index, smoother
):
    tiers, rows = lax.axis_size("tier"), lax.axis_size("row")
    count = tiers * rows
    height, k = current_modes.shape
    bt = diag_tiles.shape[-1]
    unit = 8 * count
    totals = [-(-blocks * k // unit) * unit for blocks in (6, 6, 3)]
    boxes = []
    for total in totals:
        n1 = total // 2
        n2 = n1 // (2 * tiers)
        n3 = n2 // (rows // 4)
        for shape in ((n1, k), (n2, k), (n1, k), (2 * tiers, n2, k), (rows // 4, n3, k)):
            boxes.append(pltpu.VMEM(shape, F32))
    smem = pl.BlockSpec(memory_space=pltpu.SMEM)
    hbm = pl.BlockSpec(memory_space=pltpu.HBM)
    pair = pltpu.VMEM((height, 2 * k), BF16)
    single = pltpu.VMEM((height, k), BF16)
    tall = pltpu.VMEM((height, bt), BF16)
    square = pltpu.VMEM((height, height), BF16)
    wide = pltpu.VMEM((height, k), F32)
    stacked, early, mid, late = pl.pallas_call(
        functools.partial(step_kernel, tiers, rows),
        out_shape=[
            jax.ShapeDtypeStruct((height, 3 * k), F32)] + [
            jax.ShapeDtypeStruct((total, k), F32) for total in totals],
        in_specs=[hbm, hbm, hbm, hbm, smem, hbm, smem, hbm],
        out_specs=vmem(4),
        scratch_shapes=[
            pltpu.VMEM((2, bt, bt), BF16), pltpu.VMEM((2, 2, bt, bt), BF16), pltpu.VMEM((2, bt, bt), BF16),
            pltpu.VMEM((2, bt, bt), F32), pltpu.SemaphoreType.DMA((6,)),
            pltpu.VMEM((32, bt), BF16), pltpu.VMEM((32, bt), BF16), pltpu.VMEM((2, bt, bt), BF16),
            pair, pair, pair, pair, pair,
            tall, tall, square, tall, tall, square,
            wide, wide, wide, wide, single, single, single, single, single,
            pltpu.VMEM((count, 8, k), F32),
        ] + [pltpu.VMEM((total, k), F32) for total in totals] + [
            pltpu.SemaphoreType.DMA((SEMS,)), pltpu.SemaphoreType.DMA((SEMS,))] + boxes,
        compiler_params=pltpu.CompilerParams(
            collective_id=0, has_side_effects=True, vmem_limit_bytes=60 * 2**20),
        name="step",
    )(
        current_modes, previous, diag_tiles[0, 0], lateral_tiles[0, 0], lateral_index[0, 0],
        vertical_tiles[0, 0], vertical_index[0, 0], smoother[0, 0])
    n = 3 * k
    full = pltpu.VMEM((n, n), F32)
    return pl.pallas_call(
        functools.partial(basis_kernel, 1.0 / (height * count)),
        out_shape=[jax.ShapeDtypeStruct((height, n), F32), jax.ShapeDtypeStruct((n, n), F32)],
        in_specs=vmem(4),
        out_specs=vmem(2),
        scratch_shapes=[full, full, full],
        compiler_params=pltpu.CompilerParams(vmem_limit_bytes=60 * 2**20),
        name="basis",
    )(early, mid, late, stacked)


def solution(mesh):
    placed = (
        P(("tier", "row"), None),
        P(("tier", "row"), None),
        P("tier", "row", None, None, None),
        P("tier", "row", None, None, None, None),
        P("tier", "row", None, None),
        P("tier", "row", None, None, None),
        P("tier", "row", None),
        P("tier", "row", None, None, None),
    )
    return jax.shard_map(
        on_device,
        mesh=mesh,
        in_specs=placed,
        out_specs=(P(("tier", "row"), None), P()),
        check_vma=False,
    )
```
